256 devices in a mesh: ctx: 32 (over y_hi, z, core), tp: 8 (over x, y_lo).
Axes of the slice: x: 4, y: 4 (y_hi: 2, y_lo: 2; y = y_hi * 2 + y_lo), z: 8, core: 2. Of those that a mesh axis runs over, the one named last changes fastest.
Arguments:
- student_rows: bfloat16 [8192, 8192], P('ctx', 'tp'), may hold values from -3 to 3
- queries: bfloat16 [8192, 4096], P('ctx', 'tp'), may hold values from -5 to 5
- keys_values: bfloat16 [2, 8192, 512], P(None, 'ctx'), may hold values from -5 to 5
- out_weight: bfloat16 [4096, 8192], P(None, 'tp'), may hold values from -0.09375 to 0.09375
- teacher_rows: bfloat16 [12288, 8192], P('ctx', 'tp'), may hold values from -6 to 6
- span_start: int32 [8192], P('ctx'), may hold values from 0 to 12287, as said below
- span_len: int32 [8192], P('ctx'), may hold values from 1 to 4, as said below
Outputs:
- student_out: bfloat16 [8192, 8192], P('ctx', 'tp')
- teacher_grad: bfloat16 [12288, 8192], P('ctx', 'tp')
The draws below stay inside these ranges and needn't reach their ends.
Inputs may be any that keep to these rules, and one draw needn't show every extreme that they name: Student token s of shard c = s // 256 pools teacher tokens span_start[s] to span_start[s] + span_len[s] - 1, all within 8 tokens of shard c's block of teacher tokens c * 384 to (c + 1) * 384 - 1. The first student token of every shard but the first starts exactly 8 tokens before that block. `span_len`: the last student token of every shard but the last ends exactly 8 tokens after its shard's block.
All inputs are finite; a program needn't handle non-finite values.
Results may differ from the reference program's by a relative error of at most 0.012.
Values may be sent and summed in bfloat16 or wider, within the bound.
A program may use at most 128 MiB of HBM per device.

```python
import math
import jax
import jax.numpy as jnp
from jax import lax

D = 8192
HEADS = 32
KVH = 4
HD = 128
S_DEV = 256
JIT = 3
LMAX = 4
HALO = 8
TOKENS = 8192
TD_DEV = 384
TEACH_TOKENS = 12288
N_CTX = 32


def draw_queries(key, part):
    drawn_key = jax.random.fold_in(key, 1)
    result = 2.5 * jax.random.truncated_normal(drawn_key, -2.0, 2.0, (TOKENS, HEADS, HD), jnp.float32)
    return result.reshape(TOKENS, HEADS * HD).astype(jnp.bfloat16)


def draw_keys_values(key, part):
    key_seed = jax.random.fold_in(key, 2)
    value_seed = jax.random.fold_in(key, 3)
    key_part = jax.random.truncated_normal(key_seed, -5.0, 5.0, (TOKENS, KVH, HD), jnp.float32)
    value_part = 2.0 * jax.random.truncated_normal(value_seed, -2.5, 2.5, (TOKENS, KVH, HD), jnp.float32)
    stacked = jnp.stack([key_part.reshape(TOKENS, KVH * HD), value_part.reshape(TOKENS, KVH * HD)])
    return stacked.astype(jnp.bfloat16)


def span_table(key):
    seeded = jax.random.fold_in(key, 517)
    first_key, second_key = jax.random.split(seeded)
    rows = jnp.arange(TOKENS, dtype=jnp.int32)
    local = rows % S_DEV
    shard = rows // S_DEV
    length = jax.random.randint(first_key, (TOKENS,), 1, LMAX + 1, dtype=jnp.int32)
    jitter = jax.random.randint(second_key, (TOKENS,), -JIT, JIT + 1, dtype=jnp.int32)
    start = shard * TD_DEV + local * TD_DEV // S_DEV + jitter
    start = jnp.where(local == 0, shard * TD_DEV - HALO, start)
    length = jnp.where(local == S_DEV - 1, LMAX, length)
    start = jnp.where(local == S_DEV - 1, (shard + 1) * TD_DEV + HALO - LMAX, start)
    start = jnp.clip(start, 0, TEACH_TOKENS - length)
    return (start.astype(jnp.int32), length.astype(jnp.int32))


def draw_span_start(key, part):
    return span_table(key)[0]


def draw_span_len(key, part):
    return span_table(key)[1]


def level_of(stream_key, dims, pieces, low, high):
    gain, own = 1.0, jax.random.fold_in(stream_key, 6)
    for axis_at, parts in pieces:
        steps = jnp.exp(jax.random.uniform(jax.random.fold_in(own, axis_at), (parts,), jnp.float32, low / len(pieces), high / len(pieces)))
        gain = gain * jnp.repeat(steps, dims[axis_at] // parts).reshape([-1 if axis == axis_at else 1 for axis in range(len(dims))])
    return gain


def noise(rng, dims, scale, bound, shards=(), kind=jnp.bfloat16):
    gain = level_of(rng, dims, shards, -0.22, 0.18) if shards else 1.0
    array = jax.random.normal(rng, dims, jnp.float32) * scale * gain
    return jnp.minimum(jnp.maximum(array, -bound), bound).astype(kind)


def setup_inputs(seed: int = 0) -> dict:
    key_of = jax.random.split(jax.random.key(seed), 8)
    return {
        "student_rows": noise(key_of[0], (TOKENS, D), 0.5, 3.0, ((0, 32), (1, 8))),
        "queries": draw_queries(jax.random.fold_in(key_of[7], 71), 0),
        "keys_values": draw_keys_values(jax.random.fold_in(key_of[7], 71), 0),
        "out_weight": noise(key_of[3], (HEADS * HD, D), (HEADS * HD) ** -0.5, 0.09375, ((1, 8),)),
        "teacher_rows": noise(key_of[4], (TEACH_TOKENS, D), 1.0, 6.0, ((0, 32), (1, 8))),
        "span_start": draw_span_start(jax.random.fold_in(key_of[7], 71), 0),
        "span_len": draw_span_len(jax.random.fold_in(key_of[7], 71), 0),
    }


def reference(student_rows, queries, keys_values, out_weight, teacher_rows, span_start, span_len):
    score_scale = 1.0 / math.sqrt(HD)
    group_size = HEADS // KVH
    block_rows = math.gcd(TOKENS, 512)
    block_count = TOKENS // block_rows
    query_cube = queries.reshape(TOKENS, HEADS, HD)

    def head_block(index):
        head_index = (index // block_count).astype(jnp.int32)
        block_index = (index % block_count).astype(jnp.int32)
        query_rows = lax.dynamic_slice(query_cube, (block_index * block_rows, head_index, jnp.int32(0)), (block_rows, 1, HD)).reshape(block_rows, HD)
        kv_col = (head_index // group_size * HD).astype(jnp.int32)
        key_rows = lax.dynamic_slice(keys_values[0], (jnp.int32(0), kv_col), (TOKENS, HD))
        value_rows = lax.dynamic_slice(keys_values[1], (jnp.int32(0), kv_col), (TOKENS, HD))
        scores = jnp.dot(query_rows, key_rows.T, preferred_element_type=jnp.float32) * score_scale
        query_pos = block_index * block_rows + jnp.arange(block_rows, dtype=jnp.int32)
        key_pos = jnp.arange(TOKENS, dtype=jnp.int32)
        visible = key_pos[None, :] <= query_pos[:, None]
        scores = jnp.where(visible, scores, jnp.float32(-1e+30))
        row_peak = lax.optimization_barrier(jnp.max(scores, axis=1, keepdims=True))
        weights = jnp.where(visible, jnp.exp(scores - row_peak), jnp.float32(0.0))
        row_total = lax.optimization_barrier(jnp.sum(weights, axis=1, keepdims=True))
        summed = jnp.dot(weights.astype(jnp.bfloat16), value_rows, preferred_element_type=jnp.float32)
        return (summed / row_total).astype(jnp.bfloat16)
    heads_out = lax.map(head_block, jnp.arange(HEADS * block_count, dtype=jnp.int32))
    attended = heads_out.reshape(HEADS, block_count, block_rows, HD).transpose(1, 2, 0, 3).reshape(TOKENS, HEADS * HD)
    width = TD_DEV + 2 * HALO
    padded = jnp.pad(teacher_rows, ((HALO, HALO), (0, 0)))

    def member_of(shard):
        starts = lax.dynamic_slice(span_start, (shard * S_DEV,), (S_DEV,))
        counts = lax.dynamic_slice(span_len, (shard * S_DEV,), (S_DEV,))
        columns = shard * TD_DEV - HALO + jnp.arange(width, dtype=jnp.int32)
        inside = (columns[None, :] >= starts[:, None]) & (columns[None, :] < (starts + counts)[:, None])
        return (inside.astype(jnp.bfloat16), counts.astype(jnp.float32)[:, None])

    def forward(shard):
        shard = shard.astype(jnp.int32)
        member, counts = member_of(shard)
        window = lax.dynamic_slice(padded, (shard * TD_DEV, jnp.int32(0)), (width, D))
        target = jnp.dot(member, window, preferred_element_type=jnp.float32) / counts
        attended_rows = lax.dynamic_slice(attended, (shard * S_DEV, jnp.int32(0)), (S_DEV, HEADS * HD))
        own_rows = lax.dynamic_slice(student_rows, (shard * S_DEV, jnp.int32(0)), (S_DEV, D))
        student32 = own_rows.astype(jnp.float32) + jnp.dot(attended_rows, out_weight, preferred_element_type=jnp.float32)
        resid = student32 - target
        weighted = (resid / counts).astype(jnp.bfloat16)
        return (student32.astype(jnp.bfloat16), weighted)
    outs_rows, weighted_all = lax.map(forward, jnp.arange(N_CTX, dtype=jnp.int32))
    student_out = outs_rows.reshape(TOKENS, D)

    def spread(shard):
        member, counts = member_of(shard)
        return lax.dot_general(member, weighted_all[shard], (((0,), (0,)), ((), ())), preferred_element_type=jnp.float32)

    def backward(shard):
        shard = shard.astype(jnp.int32)
        own_terms = spread(shard)
        above = spread(jnp.minimum(shard + 1, N_CTX - 1)) * (shard + 1 < N_CTX).astype(jnp.float32)
        below = spread(jnp.maximum(shard - 1, 0)) * (shard > 0).astype(jnp.float32)
        core = own_terms[HALO:HALO + TD_DEV]
        core = core.at[TD_DEV - HALO:].add(above[:HALO])
        core = core.at[:HALO].add(below[TD_DEV + HALO:])
        return core.astype(jnp.bfloat16)
    teacher_grad = lax.map(backward, jnp.arange(N_CTX, dtype=jnp.int32)).reshape(TEACH_TOKENS, D)
    return (student_out, teacher_grad)
```

```python
import functools
import math

import jax
import jax.numpy as jnp
from jax import lax
from jax.experimental import pallas as pl
from jax.experimental.pallas import tpu as pltpu
from jax.sharding import PartitionSpec as P

HD = 128
S_DEV = 256
HALO = 8
N_Z = 8
MESH = pl.DeviceIdType.MESH
EXP_SCALE = math.log2(math.e) / math.sqrt(HD)
LOW = -1e30


def pick(step, table):
    value = table[0]
    for k in range(1, len(table)):
        value = jnp.where(step == k, table[k], value)
    return value


def attend_kernel(
    q_ref, kv_ref, out_ref, buf, own_v, q_t, scores, peak, decay, total, accum,
    recv, send_right, send_left, send_sib, send_cross, send_pair, load,
):
    ctx, tp = lax.axis_index("ctx"), lax.axis_index("tp")
    core, z, y_hi = ctx % 2, (ctx // 2) % N_Z, ctx // 16
    x, y_lo = tp // 2, tp % 2
    sibling = ctx + 1 - 2 * core
    right = y_hi * 16 + ((z + 1) % N_Z) * 2 + core
    left = y_hi * 16 + ((z + N_Z - 1) % N_Z) * 2 + core
    other_hi = (ctx + 16) % 32
    pair = tp + 1 - 2 * y_lo
    kind_in, kind_swap = 1 - y_lo, y_lo

    def at(hi, steps):
        return hi * 16 + ((z + steps + N_Z) % N_Z) * 2 + core

    def swap(slot):
        return slot + 1 - 2 * core

    def part(kind, slot):
        return buf.at[kind, pl.ds(pl.multiple_of(slot * S_DEV, S_DEV), S_DEV)]

    def copy(kind, slot, to_ctx, to_tp, sem):
        return pltpu.make_async_remote_copy(
            src_ref=part(kind, slot), dst_ref=part(kind, slot), send_sem=sem,
            recv_sem=recv.at[kind, slot], device_id=(to_ctx, to_tp), device_id_type=MESH,
        )

    def arrived(kind, slot):
        copy(kind, slot, sibling, tp, send_sib.at[kind, slot]).wait_recv()

    def to_sibling(kind, slot):
        return copy(kind, slot, sibling, tp, send_sib.at[kind, slot])

    def to_right(kind, hops):
        return copy(kind, at(y_hi, -hops), right, tp, send_right.at[kind, hops])

    def to_left(kind, hops):
        return copy(kind, at(y_hi, hops), left, tp, send_left.at[kind, hops])

    def to_cross(slot):
        return copy(y_lo, slot, other_hi, pair, send_cross.at[slot // 2 % N_Z])

    def to_pair(slot):
        return copy(kind_in, slot, ctx, pair, send_pair.at[slot // 2 % N_Z])

    k_load = pltpu.make_async_copy(
        kv_ref.at[0, :, pl.ds(pl.multiple_of(x * HD, HD), HD)], part(0, ctx), load.at[0]
    )
    v_load = pltpu.make_async_copy(
        kv_ref.at[1, :, pl.ds(pl.multiple_of(x * HD, HD), HD)], own_v, load.at[1]
    )
    k_load.start()
    v_load.start()
    barrier = pltpu.get_barrier_semaphore()
    for to_ctx, to_tp in (
        (right, tp), (left, tp), (sibling, tp), (other_hi, pair), (ctx, pair),
    ):
        pl.semaphore_signal(barrier, inc=1, device_id=(to_ctx, to_tp), device_id_type=MESH)
    v_load.wait()
    v_own = own_v[...].astype(jnp.float32)
    for half in range(2):
        turned = v_own[half * HD : (half + 1) * HD].T.astype(jnp.bfloat16)
        start = pl.multiple_of(ctx * S_DEV + half * HD, HD)
        buf[1, pl.ds(start, HD), :] = turned
    k_load.wait()
    pl.semaphore_wait(barrier, 5)

    for kind in range(2):
        to_sibling(kind, ctx).start()
        to_right(kind, 0).start()
        to_left(kind, 0).start()

    @pl.when(y_hi == 0)
    def _():
        to_cross(ctx).start()

    for h in range(4):
        q_t[:, h * S_DEV : (h + 1) * S_DEV] = (
            q_ref[:, h * HD : (h + 1) * HD].astype(jnp.float32).T.astype(jnp.bfloat16)
        )

    def ring(hops):
        def side(kind, moving_right):
            slot = at(y_hi, -hops if moving_right else hops)
            arrived(kind, slot)
            last = 3 if (kind == 0) == moving_right else 2
            if hops <= last:
                (to_right if moving_right else to_left)(kind, hops).start()
            to_sibling(kind, slot).start()

            @pl.when((y_hi == 0) & (y_lo == kind))
            def _():
                to_cross(slot).start()

        if hops < 4:
            for kind in range(2):
                side(kind, True)
                side(kind, False)
        else:
            side(0, True)
            side(1, False)

    def low_slots(hops):
        if hops in (0, 4):
            return [at(0, hops)]
        return [at(0, -hops), at(0, hops)]

    def from_cross(hops):
        for slot in low_slots(hops):
            arrived(kind_in, slot)
            to_pair(slot).start()
            to_sibling(kind_in, slot).start()

    def from_pair(hops):
        for slot in low_slots(hops):
            arrived(kind_swap, slot)
            to_sibling(kind_swap, slot).start()

    half_rows = 2 * S_DEV

    def score(block, c, masked=False):
        cols = slice(c * half_rows, (c + 1) * half_rows)
        keys = buf[0, pl.ds(pl.multiple_of(block * 2 * S_DEV, 2 * S_DEV), 2 * S_DEV), :]
        s = jnp.dot(keys, q_t[:, cols], preferred_element_type=jnp.float32)
        if masked:
            key_pos = lax.broadcasted_iota(jnp.int32, s.shape, 0)
            query_pos = lax.broadcasted_iota(jnp.int32, s.shape, 1) % S_DEV + core * S_DEV
            s = jnp.where(key_pos <= query_pos, s, LOW)
        scores[c] = s
        new_peak = jnp.max(s, axis=0, keepdims=True)
        if not masked:
            old = peak[:, cols]
            new_peak = jnp.maximum(old, new_peak)
            decay[:, cols] = jnp.exp2((old - new_peak) * EXP_SCALE)
        peak[:, cols] = new_peak

    def gather_values(block, c, first=False):
        cols = slice(c * half_rows, (c + 1) * half_rows)
        weights = jnp.exp2((scores[c] - peak[:, cols]) * EXP_SCALE)
        added = jnp.sum(weights, axis=0, keepdims=True)
        rounded = weights.astype(jnp.bfloat16)
        base = block * 2 * S_DEV
        product = None
        for k in range(2):
            parts = [
                buf[1, pl.ds(pl.multiple_of(base + k * S_DEV + g * HD, HD), HD), :]
                for g in range(2)
            ]
            values = jnp.concatenate(parts, axis=1)
            term = jnp.dot(
                values, rounded[k * S_DEV : (k + 1) * S_DEV], preferred_element_type=jnp.float32
            )
            product = term if product is None else product + term
        if first:
            total[:, cols] = added
            accum[:, cols] = product
        else:
            shrink = decay[:, cols]
            total[:, cols] = total[:, cols] * shrink + added
            accum[:, cols] = accum[:, cols] * shrink + product

    own_block = ctx // 2
    for kind in range(2):
        arrived(kind, sibling)
    score(own_block, 0, masked=True)
    score(own_block, 1, masked=True)
    gather_values(own_block, 0, first=True)
    total[:, half_rows:] = jnp.zeros((1, half_rows), jnp.float32)
    accum[:, half_rows:] = jnp.zeros((HD, half_rows), jnp.float32)
    decay[:, half_rows:] = jnp.ones((1, half_rows), jnp.float32)

    events = {
        1: [(ring, 1)], 2: [(from_cross, 0)], 3: [(ring, 2), (from_pair, 0)],
        4: [(from_cross, 1)], 5: [(from_pair, 1)], 6: [(ring, 3), (from_cross, 2)],
        7: [(from_pair, 2)], 9: [(ring, 4), (from_cross, 3)], 10: [(from_pair, 3)],
        12: [(from_cross, 4)], 13: [(from_pair, 4)],
    }
    order = [
        None, ("own", -1), ("own", 1), ("own", -2), ("low", 0), ("own", 2), ("low", -1), ("own", -3),
        ("low", 1), ("own", 3), ("low", -2), ("own", 4), ("low", 2), ("low", -3), ("low", 3), ("low", 4),
    ]
    is_low = [0] + [1 if kind == "low" else 0 for kind, _ in order[1:]]
    shift = [0] + [steps for _, steps in order[1:]]

    def step(n, before):
        low = pick(n, is_low)
        block_z = (z + pick(n, shift) + N_Z) % N_Z
        for k, todo in events.items():
            for action, hops in todo:
                when = n == k
                if action is not ring:
                    when = when & (y_hi == 1)

                @pl.when(when)
                def _(action=action, hops=hops):
                    action(hops)

        block = jnp.where(low == 1, block_z, y_hi * N_Z + block_z)
        here = (low == 0) | (y_hi == 1)

        @pl.when(here)
        def _():
            for kind in range(2):
                arrived(kind, block * 2 + 1 - core)

        def compute(prior):
            score(block, 0)
            gather_values(prior, 1)
            score(block, 1)
            gather_values(block, 0)
            return block

        return lax.cond(here & (block < own_block), compute, lambda prior: prior, before)

    last_block = lax.fori_loop(1, 16, step, own_block)
    gather_values(last_block, 1)
    for h in range(4):
        cols = slice(h * S_DEV, (h + 1) * S_DEV)
        out_ref[:, h * HD : (h + 1) * HD] = (accum[:, cols] / total[:, cols]).T.astype(jnp.bfloat16)

    for kind in range(2):
        for hops in range(4 if kind == 0 else 3):
            to_right(kind, hops).wait_send()
        for hops in range(3 if kind == 0 else 4):
            to_left(kind, hops).wait_send()

    def sent(slot, _):
        for kind in range(2):
            to_sibling(kind, y_hi * 16 + slot * 2 + core).wait_send()

        @pl.when(y_hi == 0)
        def _():
            to_cross(slot * 2 + core).wait_send()

        @pl.when(y_hi == 1)
        def _():
            to_pair(slot * 2 + core).wait_send()
            for kind in range(2):
                to_sibling(kind, slot * 2 + core).wait_send()

        return 0

    lax.fori_loop(0, N_Z, sent, 0)


def attention(queries, keys_values):
    rows = queries.shape[0]
    wide = 4 * rows
    return pl.pallas_call(
        attend_kernel,
        out_shape=jax.ShapeDtypeStruct(queries.shape, jnp.bfloat16),
        in_specs=[pl.BlockSpec(memory_space=pltpu.VMEM), pl.BlockSpec(memory_space=pl.ANY)],
        out_specs=pl.BlockSpec(memory_space=pltpu.VMEM),
        scratch_shapes=[
            pltpu.VMEM((2, 32 * S_DEV, HD), jnp.bfloat16),
            pltpu.VMEM((S_DEV, HD), jnp.bfloat16),
            pltpu.VMEM((HD, wide), jnp.bfloat16),
            pltpu.VMEM((2, 2 * S_DEV, wide // 2), jnp.float32),
            pltpu.VMEM((1, wide), jnp.float32),
            pltpu.VMEM((1, wide), jnp.float32),
            pltpu.VMEM((1, wide), jnp.float32),
            pltpu.VMEM((HD, wide), jnp.float32),
            pltpu.SemaphoreType.DMA((2, 32)),
            pltpu.SemaphoreType.DMA((2, 4)),
            pltpu.SemaphoreType.DMA((2, 4)),
            pltpu.SemaphoreType.DMA((2, 32)),
            pltpu.SemaphoreType.DMA((N_Z,)),
            pltpu.SemaphoreType.DMA((N_Z,)),
            pltpu.SemaphoreType.DMA((2,)),
        ],
        compiler_params=pltpu.CompilerParams(
            collective_id=0, has_side_effects=True, vmem_limit_bytes=40 << 20
        ),
        name="attention",
    )(queries, keys_values)


def with_halo(array, sides, width):
    for axis, dim in sides:
        peers, length = (lax.axis_size(axis), array.shape[dim])
        up = [(i, (i + 1) % peers) for i in range(peers - 1)]
        down = [(j, i) for i, j in up]
        last = lax.slice_in_dim(array, length - width, length, axis=dim)
        leading = lax.slice_in_dim(array, 0, width, axis=dim)
        before = lax.ppermute(last, axis, up)
        after = lax.ppermute(leading, axis, down)
        array = jnp.concatenate([before, array, after], axis=dim)
    return array


def in_order(blocks, dim):
    shape = list(blocks.shape[1:])
    shape[dim] *= blocks.shape[0]
    return jnp.moveaxis(blocks, 0, dim).reshape(shape)


def sent_to_all(array, axis):
    peers = lax.axis_size(axis)
    return lax.all_to_all(
        jnp.broadcast_to(array[None], (peers, *array.shape)), axis, 0, 0, tiled=True
    )


def collect(array, axis, dim):
    blocks = sent_to_all(array, axis)
    return in_order(blocks, dim)


def shifted(value, axis, steps):
    count = lax.axis_size(axis)
    leading, last = (max(0, -steps), min(count, count - steps))
    return lax.ppermute(value, axis, [(source, source + steps) for source in range(leading, last)])


def body(student_rows, queries, keys_values, out_weight, teacher_rows, span_start, span_len):
    ctx_rank = lax.axis_index("ctx")
    teach_dev = teacher_rows.shape[0]
    extended = with_halo(teacher_rows, (("ctx", 0),), HALO)
    window = teach_dev + 2 * HALO
    columns = ctx_rank * teach_dev - HALO + jnp.arange(window)
    span_end = span_start + span_len
    member = (
        (columns[None, :] >= span_start[:, None]) & (columns[None, :] < span_end[:, None])
    ).astype(jnp.bfloat16)
    span_counts = span_len.astype(jnp.float32)[:, None]
    target = jnp.dot(member, extended, preferred_element_type=jnp.float32) / span_counts
    attended = attention(queries, keys_values)
    projected = jnp.dot(collect(attended, "tp", 1), out_weight, preferred_element_type=jnp.float32)
    student32 = student_rows.astype(jnp.float32) + projected
    resid = student32 - target
    weighted = (resid / span_counts).astype(jnp.bfloat16)
    spread = lax.dot_general(
        member, weighted, (((0,), (0,)), ((), ())), preferred_element_type=jnp.float32
    )
    from_above = shifted(spread[:HALO].astype(jnp.bfloat16), "ctx", -1).astype(jnp.float32)
    from_below = shifted(spread[teach_dev + HALO :].astype(jnp.bfloat16), "ctx", 1).astype(
        jnp.float32
    )
    core = spread[HALO : HALO + teach_dev]
    core = core.at[teach_dev - HALO :].add(from_above)
    core = core.at[:HALO].add(from_below)
    return (student32.astype(jnp.bfloat16), core.astype(jnp.bfloat16))


def solution(mesh):
    return jax.shard_map(
        body,
        mesh=mesh,
        in_specs=(
            P("ctx", "tp"),
            P("ctx", "tp"),
            P(None, "ctx", None),
            P(None, "tp"),
            P("ctx", "tp"),
            P("ctx"),
            P("ctx"),
        ),
        out_specs=(P("ctx", "tp"), P("ctx", "tp")),
        check_vma=False,
    )
```

```python
import functools
import math

import jax
import jax.numpy as jnp
from jax import lax
from jax.experimental import pallas as pl
from jax.experimental.pallas import tpu as pltpu
from jax.sharding import PartitionSpec as P

HD = 128
S_DEV = 256
HALO = 8
N_Z = 8
MESH = pl.DeviceIdType.MESH
EXP_SCALE = math.log2(math.e) / math.sqrt(HD)
LOW = -1e30

TEACH = 384
EDGE = 16
WINDOW = TEACH + 2 * EDGE
DEPTH = 512
WIDTH = 1024
QUARTER = S_DEV // 4
TILE = 256


def pick(step, table):
    value = table[0]
    for k in range(1, len(table)):
        value = jnp.where(step == k, table[k], value)
    return value


def attend_kernel(
    q_ref, kv_ref, out_ref, buf, own_v, q_t, scores, peak, decay, total, accum,
    recv, send_right, send_left, send_sib, send_cross, send_pair, load,
):
    ctx, tp = lax.axis_index("ctx"), lax.axis_index("tp")
    core, z, y_hi = ctx % 2, (ctx // 2) % N_Z, ctx // 16
    x, y_lo = tp // 2, tp % 2
    sibling = ctx + 1 - 2 * core
    right = y_hi * 16 + ((z + 1) % N_Z) * 2 + core
    left = y_hi * 16 + ((z + N_Z - 1) % N_Z) * 2 + core
    other_hi = (ctx + 16) % 32
    pair = tp + 1 - 2 * y_lo
    kind_in, kind_swap = 1 - y_lo, y_lo

    def at(hi, steps):
        return hi * 16 + ((z + steps + N_Z) % N_Z) * 2 + core

    def swap(slot):
        return slot + 1 - 2 * core

    def part(kind, slot):
        return buf.at[kind, pl.ds(pl.multiple_of(slot * S_DEV, S_DEV), S_DEV)]

    def copy(kind, slot, to_ctx, to_tp, sem):
        return pltpu.make_async_remote_copy(
            src_ref=part(kind, slot), dst_ref=part(kind, slot), send_sem=sem,
            recv_sem=recv.at[kind, slot], device_id=(to_ctx, to_tp), device_id_type=MESH,
        )

    def arrived(kind, slot):
        copy(kind, slot, sibling, tp, send_sib.at[kind, slot]).wait_recv()

    def to_sibling(kind, slot):
        return copy(kind, slot, sibling, tp, send_sib.at[kind, slot])

    def to_right(kind, hops):
        return copy(kind, at(y_hi, -hops), right, tp, send_right.at[kind, hops])

    def to_left(kind, hops):
        return copy(kind, at(y_hi, hops), left, tp, send_left.at[kind, hops])

    def to_cross(slot):
        return copy(y_lo, slot, other_hi, pair, send_cross.at[slot // 2 % N_Z])

    def to_pair(slot):
        return copy(kind_in, slot, ctx, pair, send_pair.at[slot // 2 % N_Z])

    k_load = pltpu.make_async_copy(
        kv_ref.at[0, :, pl.ds(pl.multiple_of(x * HD, HD), HD)], part(0, ctx), load.at[0]
    )
    v_load = pltpu.make_async_copy(
        kv_ref.at[1, :, pl.ds(pl.multiple_of(x * HD, HD), HD)], own_v, load.at[1]
    )
    k_load.start()
    v_load.start()
    barrier = pltpu.get_barrier_semaphore()
    for to_ctx, to_tp in (
        (right, tp), (left, tp), (sibling, tp), (other_hi, pair), (ctx, pair),
    ):
        pl.semaphore_signal(barrier, inc=1, device_id=(to_ctx, to_tp), device_id_type=MESH)
    v_load.wait()
    v_own = own_v[...].astype(jnp.float32)
    for half in range(2):
        turned = v_own[half * HD : (half + 1) * HD].T.astype(jnp.bfloat16)
        start = pl.multiple_of(ctx * S_DEV + half * HD, HD)
        buf[1, pl.ds(start, HD), :] = turned
    k_load.wait()
    pl.semaphore_wait(barrier, 5)

    for kind in range(2):
        to_sibling(kind, ctx).start()
        to_right(kind, 0).start()
        to_left(kind, 0).start()

    @pl.when(y_hi == 0)
    def _():
        to_cross(ctx).start()

    for h in range(4):
        q_t[:, h * S_DEV : (h + 1) * S_DEV] = (
            q_ref[:, h * HD : (h + 1) * HD].astype(jnp.float32).T.astype(jnp.bfloat16)
        )

    def ring(hops):
        def side(kind, moving_right):
            slot = at(y_hi, -hops if moving_right else hops)
            arrived(kind, slot)
            last = 3 if (kind == 0) == moving_right else 2
            if hops <= last:
                (to_right if moving_right else to_left)(kind, hops).start()
            to_sibling(kind, slot).start()

            @pl.when((y_hi == 0) & (y_lo == kind))
            def _():
                to_cross(slot).start()

        if hops < 4:
            for kind in range(2):
                side(kind, True)
                side(kind, False)
        else:
            side(0, True)
            side(1, False)

    def low_slots(hops):
        if hops in (0, 4):
            return [at(0, hops)]
        return [at(0, -hops), at(0, hops)]

    def from_cross(hops):
        for slot in low_slots(hops):
            arrived(kind_in, slot)
            to_pair(slot).start()
            to_sibling(kind_in, slot).start()

    def from_pair(hops):
        for slot in low_slots(hops):
            arrived(kind_swap, slot)
            to_sibling(kind_swap, slot).start()

    half_rows = 2 * S_DEV

    def score(block, c, masked=False):
        cols = slice(c * half_rows, (c + 1) * half_rows)
        keys = buf[0, pl.ds(pl.multiple_of(block * 2 * S_DEV, 2 * S_DEV), 2 * S_DEV), :]
        s = jnp.dot(keys, q_t[:, cols], preferred_element_type=jnp.float32)
        if masked:
            key_pos = lax.broadcasted_iota(jnp.int32, s.shape, 0)
            query_pos = lax.broadcasted_iota(jnp.int32, s.shape, 1) % S_DEV + core * S_DEV
            s = jnp.where(key_pos <= query_pos, s, LOW)
        scores[c] = s
        new_peak = jnp.max(s, axis=0, keepdims=True)
        if not masked:
            old = peak[:, cols]
            new_peak = jnp.maximum(old, new_peak)
            decay[:, cols] = jnp.exp2((old - new_peak) * EXP_SCALE)
        peak[:, cols] = new_peak

    def gather_values(block, c, first=False):
        cols = slice(c * half_rows, (c + 1) * half_rows)
        weights = jnp.exp2((scores[c] - peak[:, cols]) * EXP_SCALE)
        added = jnp.sum(weights, axis=0, keepdims=True)
        rounded = weights.astype(jnp.bfloat16)
        base = block * 2 * S_DEV
        product = None
        for k in range(2):
            parts = [
                buf[1, pl.ds(pl.multiple_of(base + k * S_DEV + g * HD, HD), HD), :]
                for g in range(2)
            ]
            values = jnp.concatenate(parts, axis=1)
            term = jnp.dot(
                values, rounded[k * S_DEV : (k + 1) * S_DEV], preferred_element_type=jnp.float32
            )
            product = term if product is None else product + term
        if first:
            total[:, cols] = added
            accum[:, cols] = product
        else:
            shrink = decay[:, cols]
            total[:, cols] = total[:, cols] * shrink + added
            accum[:, cols] = accum[:, cols] * shrink + product

    own_block = ctx // 2
    for kind in range(2):
        arrived(kind, sibling)
    score(own_block, 0, masked=True)
    score(own_block, 1, masked=True)
    gather_values(own_block, 0, first=True)
    total[:, half_rows:] = jnp.zeros((1, half_rows), jnp.float32)
    accum[:, half_rows:] = jnp.zeros((HD, half_rows), jnp.float32)
    decay[:, half_rows:] = jnp.ones((1, half_rows), jnp.float32)

    events = {
        1: [(ring, 1)], 2: [(from_cross, 0)], 3: [(ring, 2), (from_pair, 0)],
        4: [(from_cross, 1)], 5: [(from_pair, 1)], 6: [(ring, 3), (from_cross, 2)],
        7: [(from_pair, 2)], 9: [(ring, 4), (from_cross, 3)], 10: [(from_pair, 3)],
        12: [(from_cross, 4)], 13: [(from_pair, 4)],
    }
    order = [
        None, ("own", -1), ("own", 1), ("own", -2), ("low", 0), ("own", 2), ("low", -1), ("own", -3),
        ("low", 1), ("own", 3), ("low", -2), ("own", 4), ("low", 2), ("low", -3), ("low", 3), ("low", 4),
    ]
    is_low = [0] + [1 if kind == "low" else 0 for kind, _ in order[1:]]
    shift = [0] + [steps for _, steps in order[1:]]

    def step(n, before):
        low = pick(n, is_low)
        block_z = (z + pick(n, shift) + N_Z) % N_Z
        for k, todo in events.items():
            for action, hops in todo:
                when = n == k
                if action is not ring:
                    when = when & (y_hi == 1)

                @pl.when(when)
                def _(action=action, hops=hops):
                    action(hops)

        block = jnp.where(low == 1, block_z, y_hi * N_Z + block_z)
        here = (low == 0) | (y_hi == 1)

        @pl.when(here)
        def _():
            for kind in range(2):
                arrived(kind, block * 2 + 1 - core)

        def compute(prior):
            score(block, 0)
            gather_values(prior, 1)
            score(block, 1)
            gather_values(block, 0)
            return block

        return lax.cond(here & (block < own_block), compute, lambda prior: prior, before)

    last_block = lax.fori_loop(1, 16, step, own_block)
    gather_values(last_block, 1)
    for h in range(4):
        cols = slice(h * S_DEV, (h + 1) * S_DEV)
        out_ref[:, h * HD : (h + 1) * HD] = (accum[:, cols] / total[:, cols]).T.astype(jnp.bfloat16)

    for kind in range(2):
        for hops in range(4 if kind == 0 else 3):
            to_right(kind, hops).wait_send()
        for hops in range(3 if kind == 0 else 4):
            to_left(kind, hops).wait_send()

    def sent(slot, _):
        for kind in range(2):
            to_sibling(kind, y_hi * 16 + slot * 2 + core).wait_send()

        @pl.when(y_hi == 0)
        def _():
            to_cross(slot * 2 + core).wait_send()

        @pl.when(y_hi == 1)
        def _():
            to_pair(slot * 2 + core).wait_send()
            for kind in range(2):
                to_sibling(kind, slot * 2 + core).wait_send()

        return 0

    lax.fori_loop(0, N_Z, sent, 0)


def attention(queries, keys_values):
    rows = queries.shape[0]
    wide = 4 * rows
    return pl.pallas_call(
        attend_kernel,
        out_shape=jax.ShapeDtypeStruct(queries.shape, jnp.bfloat16),
        in_specs=[pl.BlockSpec(memory_space=pltpu.VMEM), pl.BlockSpec(memory_space=pl.ANY)],
        out_specs=pl.BlockSpec(memory_space=pltpu.VMEM),
        scratch_shapes=[
            pltpu.VMEM((2, 32 * S_DEV, HD), jnp.bfloat16),
            pltpu.VMEM((S_DEV, HD), jnp.bfloat16),
            pltpu.VMEM((HD, wide), jnp.bfloat16),
            pltpu.VMEM((2, 2 * S_DEV, wide // 2), jnp.float32),
            pltpu.VMEM((1, wide), jnp.float32),
            pltpu.VMEM((1, wide), jnp.float32),
            pltpu.VMEM((1, wide), jnp.float32),
            pltpu.VMEM((HD, wide), jnp.float32),
            pltpu.SemaphoreType.DMA((2, 32)),
            pltpu.SemaphoreType.DMA((2, 4)),
            pltpu.SemaphoreType.DMA((2, 4)),
            pltpu.SemaphoreType.DMA((2, 32)),
            pltpu.SemaphoreType.DMA((N_Z,)),
            pltpu.SemaphoreType.DMA((N_Z,)),
            pltpu.SemaphoreType.DMA((2,)),
        ],
        compiler_params=pltpu.CompilerParams(
            collective_id=0, has_side_effects=True, vmem_limit_bytes=60 << 20
        ),
        name="attention",
    )(queries, keys_values)


def project_kernel(
    att_ref, student_ref, weight_ref, teacher_ref, start_ref, len_ref, out_ref, grad_ref,
    att, weight, student, ext, member, member_t, accum, target, counts, edges, landed,
    recv, send_right, send_left, send_pair, load, load_weight, edge_send, edge_recv,
):
    ctx, tp = lax.axis_index("ctx"), lax.axis_index("tp")
    x, y_lo = tp // 2, tp % 2
    pair = tp + 1 - 2 * y_lo
    right, left = ((x + 1) % 4) * 2 + y_lo, ((x + 3) % 4) * 2 + y_lo
    above, below = (ctx + 1) % 32, (ctx + 31) % 32

    def slot_at(steps, same):
        return ((x + steps + 4) % 4) * 2 + (y_lo if same else 1 - y_lo)

    def piece(slot, q):
        return att.at[slot, pl.ds(q * QUARTER, QUARTER)]

    def copy(slot, q, to_tp, sems):
        return pltpu.make_async_remote_copy(
            src_ref=piece(slot, q), dst_ref=piece(slot, q), send_sem=sems.at[slot, q],
            recv_sem=recv.at[slot, q], device_id=(ctx, to_tp), device_id_type=MESH,
        )

    to_right = lambda slot, q: copy(slot, q, right, send_right)
    to_left = lambda slot, q: copy(slot, q, left, send_left)
    to_pair = lambda slot, q: copy(slot, q, pair, send_pair)

    def arrived(slot, q):
        to_pair(slot, q).wait_recv()

    def edge_copy(k):
        to_ctx = above if k == 0 else below
        src = teacher_ref.at[pl.ds(TEACH - EDGE, EDGE)] if k == 0 else teacher_ref.at[pl.ds(0, EDGE)]
        dst = ext.at[pl.ds(0, EDGE)] if k == 0 else ext.at[pl.ds(EDGE + TEACH, EDGE)]
        return pltpu.make_async_remote_copy(
            src_ref=src, dst_ref=dst, send_sem=edge_send.at[k], recv_sem=edge_recv.at[k],
            device_id=(to_ctx, tp), device_id_type=MESH,
        )

    def grad_copy(k):
        return pltpu.make_async_remote_copy(
            src_ref=edges.at[k], dst_ref=landed.at[k], send_sem=edge_send.at[2 + k],
            recv_sem=edge_recv.at[2 + k], device_id=(above if k == 0 else below, tp),
            device_id_type=MESH,
        )

    def weight_load(slot):
        rows = pl.ds(pl.multiple_of(slot * DEPTH, DEPTH), DEPTH)
        return pltpu.make_async_copy(weight_ref.at[rows], weight.at[rows], load_weight.at[slot])

    own_load = pltpu.make_async_copy(att_ref, att.at[tp], load.at[0])
    student_load = pltpu.make_async_copy(student_ref, student, load.at[1])
    teacher_load = pltpu.make_async_copy(teacher_ref, ext.at[pl.ds(EDGE, TEACH)], load.at[2])
    own_load.start()
    barrier = pltpu.get_barrier_semaphore()
    for to_ctx, to_tp in ((ctx, right), (ctx, left), (ctx, pair), (above, tp), (below, tp)):
        pl.semaphore_signal(barrier, inc=1, device_id=(to_ctx, to_tp), device_id_type=MESH)
    own_load.wait()
    pl.semaphore_wait(barrier, 5)

    for k in range(4):
        to_pair(tp, (2, 3, 0, 1)[k]).start()
        to_right(tp, (0, 2, 1, 3)[k]).start()
        to_left(tp, (1, 3, 0, 2)[k]).start()
    for k in range(2):
        edge_copy(k).start()
    student_load.start()
    teacher_load.start()
    order = [
        tp, pair, slot_at(-1, True), slot_at(1, True), slot_at(2, True),
        slot_at(-1, False), slot_at(1, False), slot_at(2, False),
    ]
    for slot in order:
        weight_load(slot).start()

    ext[WINDOW:, :] = jnp.zeros((ext.shape[0] - WINDOW, WIDTH), jnp.bfloat16)
    first = ctx * TEACH - EDGE
    start_row, len_row = start_ref[...], len_ref[...]
    row_pos = first + lax.broadcasted_iota(jnp.int32, (WINDOW, S_DEV), 0)
    inside = (row_pos >= start_row) & (row_pos < start_row + len_row)
    member_t[...] = jnp.where(inside, 1.0, 0.0).astype(jnp.bfloat16)
    wide_start = jnp.broadcast_to(start_row.astype(jnp.float32), (HD, S_DEV)).T[:, :1]
    wide_len = jnp.broadcast_to(len_row.astype(jnp.float32), (HD, S_DEV)).T
    counts[...] = 1.0 / wide_len
    col_pos = (first + lax.broadcasted_iota(jnp.int32, member.shape, 1)).astype(jnp.float32)
    inside = (col_pos >= wide_start) & (col_pos < wide_start + wide_len[:, :1])
    member[...] = jnp.where(inside, 1.0, 0.0).astype(jnp.bfloat16)
    student_load.wait()
    accum[...] = student[...].astype(jnp.float32)

    def columns(j):
        return pl.ds(pl.multiple_of(j * TILE, TILE), TILE)

    def multiply(slot):
        weight_load(slot).wait()
        rows = pl.ds(pl.multiple_of(slot * DEPTH, DEPTH), DEPTH)

        @pl.loop(0, WIDTH // TILE)
        def _(j):
            accum[:, columns(j)] += jnp.dot(
                att[slot], weight[rows, columns(j)], preferred_element_type=jnp.float32
            )

    prev, nxt = slot_at(-1, True), slot_at(1, True)
    far, far_other = slot_at(2, True), slot_at(2, False)
    prev_other, nxt_other = slot_at(-1, False), slot_at(1, False)

    arrived(pair, 2)
    to_right(pair, 2).start()
    to_left(pair, 2).start()
    arrived(pair, 3)
    to_left(pair, 3).start()
    to_right(pair, 3).start()
    multiply(tp)
    arrived(prev, 0)
    to_right(prev, 0).start()
    to_pair(prev, 0).start()
    arrived(nxt, 1)
    to_left(nxt, 1).start()
    to_pair(nxt, 1).start()
    arrived(prev, 2)
    to_right(prev, 2).start()
    arrived(nxt, 3)
    to_left(nxt, 3).start()
    arrived(prev, 1)
    to_pair(prev, 1).start()
    arrived(nxt, 0)
    to_pair(nxt, 0).start()
    teacher_load.wait()
    for k in range(2):
        edge_copy(k).wait_recv()

    @pl.loop(0, WIDTH // TILE)
    def _(j):
        summed = jnp.dot(member[...], ext[:, columns(j)], preferred_element_type=jnp.float32)
        target[:, columns(j)] = summed * counts[:, :1]

    arrived(pair, 0)
    arrived(pair, 1)
    arrived(prev_other, 2)
    to_right(prev_other, 2).start()
    arrived(nxt_other, 3)
    to_left(nxt_other, 3).start()
    multiply(pair)
    arrived(far, 0)
    to_pair(far, 0).start()
    arrived(far, 1)
    to_pair(far, 1).start()
    arrived(prev, 3)
    multiply(prev)
    arrived(nxt, 2)
    multiply(nxt)
    for q in (2, 3):
        arrived(far, q)
    multiply(far)
    for q in (3, 0, 1):
        arrived(prev_other, q)
    multiply(prev_other)
    for q in (2, 0, 1):
        arrived(nxt_other, q)
    multiply(nxt_other)
    for q in (2, 3, 0, 1):
        arrived(far_other, q)
    weight_load(far_other).wait()
    last_rows = pl.ds(pl.multiple_of(far_other * DEPTH, DEPTH), DEPTH)

    @pl.loop(0, WIDTH // TILE)
    def _(j):
        student32 = accum[:, columns(j)] + jnp.dot(
            att[far_other], weight[last_rows, columns(j)], preferred_element_type=jnp.float32
        )
        out_ref[:, columns(j)] = student32.astype(jnp.bfloat16)
        weighted = ((student32 - target[:, columns(j)]) * counts[:, :1]).astype(jnp.bfloat16)
        spread = jnp.dot(member_t[...], weighted, preferred_element_type=jnp.float32)
        edges[0, :, columns(j)] = spread[EDGE + TEACH : EDGE + TEACH + HALO]
        edges[1, :, columns(j)] = spread[EDGE - HALO : EDGE]
        accum[:, columns(j)] = spread[EDGE : EDGE + S_DEV]
        target[: TEACH - S_DEV, columns(j)] = spread[EDGE + S_DEV : EDGE + TEACH]

    for k in range(2):
        grad_copy(k).start()
    grad_ref[EDGE:S_DEV, :] = accum[EDGE:, :].astype(jnp.bfloat16)
    rest = TEACH - S_DEV - EDGE
    grad_ref[S_DEV : TEACH - EDGE, :] = target[:rest, :].astype(jnp.bfloat16)
    for k in range(2):
        grad_copy(k).wait_recv()
    low = accum[:EDGE, :] + jnp.concatenate([landed[0], jnp.zeros_like(landed[0])], axis=0)
    grad_ref[:EDGE, :] = low.astype(jnp.bfloat16)
    high = target[rest : rest + EDGE, :] + jnp.concatenate(
        [jnp.zeros_like(landed[1]), landed[1]], axis=0
    )
    grad_ref[TEACH - EDGE :, :] = high.astype(jnp.bfloat16)

    for k in range(2):
        edge_copy(k).wait_send()
        grad_copy(k).wait_send()
    for q in range(4):
        to_pair(tp, q).wait_send()
        to_right(tp, q).wait_send()
        to_left(tp, q).wait_send()
    for q in (2, 3):
        to_right(pair, q).wait_send()
        to_left(pair, q).wait_send()
    for slot, q in ((prev, 0), (prev, 2), (prev_other, 2)):
        to_right(slot, q).wait_send()
    for slot, q in ((nxt, 1), (nxt, 3), (nxt_other, 3)):
        to_left(slot, q).wait_send()
    for slot in (prev, nxt, far):
        for q in range(2):
            to_pair(slot, q).wait_send()


def body(student_rows, queries, keys_values, out_weight, teacher_rows, span_start, span_len):
    attended = attention(queries, keys_values)
    in_vmem, anywhere = pl.BlockSpec(memory_space=pltpu.VMEM), pl.BlockSpec(memory_space=pl.ANY)
    dma = pltpu.SemaphoreType.DMA
    return pl.pallas_call(
        project_kernel,
        out_shape=(
            jax.ShapeDtypeStruct((S_DEV, WIDTH), jnp.bfloat16),
            jax.ShapeDtypeStruct((TEACH, WIDTH), jnp.bfloat16),
        ),
        in_specs=[anywhere, anywhere, anywhere, anywhere, in_vmem, in_vmem],
        out_specs=(in_vmem, in_vmem),
        scratch_shapes=[
            pltpu.VMEM((8, S_DEV, DEPTH), jnp.bfloat16),
            pltpu.VMEM((8 * DEPTH, WIDTH), jnp.bfloat16),
            pltpu.VMEM((S_DEV, WIDTH), jnp.bfloat16),
            pltpu.VMEM((512, WIDTH), jnp.bfloat16),
            pltpu.VMEM((S_DEV, 512), jnp.bfloat16),
            pltpu.VMEM((WINDOW, S_DEV), jnp.bfloat16),
            pltpu.VMEM((S_DEV, WIDTH), jnp.float32),
            pltpu.VMEM((S_DEV, WIDTH), jnp.float32),
            pltpu.VMEM((S_DEV, HD), jnp.float32),
            pltpu.VMEM((2, HALO, WIDTH), jnp.float32),
            pltpu.VMEM((2, HALO, WIDTH), jnp.float32),
            dma((8, 4)), dma((8, 4)), dma((8, 4)), dma((8, 4)), dma((3,)), dma((8,)), dma((4,)), dma((4,)),
        ],
        compiler_params=pltpu.CompilerParams(
            collective_id=1, has_side_effects=True, vmem_limit_bytes=60 << 20
        ),
        name="project",
    )(
        attended, student_rows, out_weight, teacher_rows,
        span_start.reshape(1, S_DEV), span_len.reshape(1, S_DEV),
    )


def solution(mesh):
    return jax.shard_map(
        body,
        mesh=mesh,
        in_specs=(
            P("ctx", "tp"),
            P("ctx", "tp"),
            P(None, "ctx", None),
            P(None, "tp"),
            P("ctx", "tp"),
            P("ctx"),
            P("ctx"),
        ),
        out_specs=(P("ctx", "tp"), P("ctx", "tp")),
        check_vma=False,
    )
```

```python
import functools
import math

import jax
import jax.numpy as jnp
from jax import lax
from jax.experimental import pallas as pl
from jax.experimental.pallas import tpu as pltpu
from jax.sharding import PartitionSpec as P

HD = 128
S_DEV = 256
HALO = 8
N_Z = 8
MESH = pl.DeviceIdType.MESH
EXP_SCALE = math.log2(math.e) / math.sqrt(HD)
LOW = -1e30

TEACH = 384
EDGE = 16
WINDOW = TEACH + 2 * EDGE
DEPTH = 512
WIDTH = 1024
QUARTER = S_DEV // 4
TILE = 256


def pick(step, table):
    value = table[0]
    for k in range(1, len(table)):
        value = jnp.where(step == k, table[k], value)
    return value


def layer_kernel(
    q_ref, kv_ref, student_ref, weight_ref, teacher_ref, start_ref, len_ref, out_ref, grad_ref,
    buf, own_v, q_rows, q_t, scores, peak, decay, total, accum,
    att, weight, student, ext, member, member_t, result, target, counts, edges, landed,
    recv, recv_sib, send_right, send_left, send_sib, send_cross, send_pair,
    x_recv, x_send_right, x_send_left, x_send_pair, load, load_weight, edge_send, edge_recv,
):
    ctx, tp = lax.axis_index("ctx"), lax.axis_index("tp")
    core, z, y_hi = ctx % 2, (ctx // 2) % N_Z, ctx // 16
    x, y_lo = tp // 2, tp % 2
    sibling = ctx + 1 - 2 * core
    right = y_hi * 16 + ((z + 1) % N_Z) * 2 + core
    left = y_hi * 16 + ((z + N_Z - 1) % N_Z) * 2 + core
    other_hi = (ctx + 16) % 32
    pair = tp + 1 - 2 * y_lo
    kind_on = jnp.where(y_hi == 0, y_lo, 1 - y_lo)
    kind_swap = 1 - kind_on
    x_right, x_left = ((x + 1) % 4) * 2 + y_lo, ((x + 3) % 4) * 2 + y_lo
    above, below = (ctx + 1) % 32, (ctx + 31) % 32

    def at(hi, steps):
        return hi * 16 + ((z + steps + N_Z) % N_Z) * 2 + core

    def piece(kind, slot, p):
        return buf.at[kind, pl.ds(pl.multiple_of(slot * S_DEV + p * HD, HD), HD)]

    def part(kind, slot):
        return buf.at[kind, pl.ds(pl.multiple_of(slot * S_DEV, S_DEV), S_DEV)]

    def copy(kind, slot, p, to_ctx, to_tp, sem):
        return pltpu.make_async_remote_copy(
            src_ref=piece(kind, slot, p), dst_ref=piece(kind, slot, p), send_sem=sem,
            recv_sem=recv.at[kind, slot * 2 + p], device_id=(to_ctx, to_tp), device_id_type=MESH,
        )

    def arrived(kind, slot, p):
        copy(kind, slot, p, ctx, pair, send_pair.at[0]).wait_recv()

    def to_sibling(kind, slot):
        return pltpu.make_async_remote_copy(
            src_ref=part(kind, slot), dst_ref=part(kind, slot), send_sem=send_sib.at[kind, slot],
            recv_sem=recv_sib.at[kind, slot], device_id=(sibling, tp), device_id_type=MESH,
        )

    def to_right(kind, hops, p):
        return copy(kind, at(y_hi, -hops), p, right, tp, send_right.at[kind, hops * 2 + p])

    def to_left(kind, hops, p):
        return copy(kind, at(y_hi, hops), p, left, tp, send_left.at[kind, hops * 2 + p])

    def to_cross(slot, p):
        return copy(y_lo, slot, p, other_hi, pair, send_cross.at[slot // 2 % N_Z * 2 + p])

    def to_pair(slot, p):
        return copy(kind_on, slot, p, ctx, pair, send_pair.at[slot // 2 % N_Z * 2 + p])

    k_load = pltpu.make_async_copy(
        kv_ref.at[0, :, pl.ds(pl.multiple_of(x * HD, HD), HD)], part(0, ctx), load.at[3]
    )
    v_load = pltpu.make_async_copy(
        kv_ref.at[1, :, pl.ds(pl.multiple_of(x * HD, HD), HD)], own_v, load.at[0]
    )
    q_load = pltpu.make_async_copy(q_ref, q_rows, load.at[4])
    v_load.start()
    k_load.start()
    q_load.start()
    barrier = pltpu.get_barrier_semaphore()
    for to_ctx, to_tp in (
        (right, tp), (left, tp), (sibling, tp), (other_hi, pair), (ctx, pair),
        (ctx, x_right), (ctx, x_left), (above, tp), (below, tp),
    ):
        pl.semaphore_signal(barrier, inc=1, device_id=(to_ctx, to_tp), device_id_type=MESH)
    v_load.wait()
    v_own = own_v[...].astype(jnp.float32)
    for half in range(2):
        turned = v_own[half * HD : (half + 1) * HD].T.astype(jnp.bfloat16)
        start = pl.multiple_of(ctx * S_DEV + half * HD, HD)
        buf[1, pl.ds(start, HD), :] = turned
    q_load.wait()
    for h in range(4):
        q_t[:, h * S_DEV : (h + 1) * S_DEV] = (
            q_rows[:, h * HD : (h + 1) * HD].astype(jnp.float32).T.astype(jnp.bfloat16)
        )
    k_load.wait()
    pl.semaphore_wait(barrier, 9)

    def for_ring(action):
        @pl.when(y_hi == 0)
        def _():
            action([y_lo])

        @pl.when(y_hi == 1)
        def _():
            action([0, 1])

    def start_own(kinds):
        for p in range(2):
            for kind in kinds:
                to_right(kind, 0, p).start()
                to_left(kind, 0, 1 - p).start()
            if len(kinds) == 1:
                to_cross(ctx, p).start()

    for_ring(start_own)
    for kind in range(2):
        to_sibling(kind, ctx).start()

    def ring(hops, kinds):
        def side(kind, moving_right, p):
            slot = at(y_hi, -hops if moving_right else hops)
            arrived(kind, slot, p)
            last = 3 if (p == 0) == moving_right else 2
            if hops <= last:
                (to_right if moving_right else to_left)(kind, hops, p).start()
            if len(kinds) == 1:
                to_cross(slot, p).start()
                to_pair(slot, p).start()

        if hops < 4:
            for k in range(2):
                for kind in kinds:
                    side(kind, True, k)
                    side(kind, False, 1 - k)
            for kind in kinds:
                to_sibling(kind, at(y_hi, -hops)).start()
                to_sibling(kind, at(y_hi, hops)).start()
        else:
            for kind in kinds:
                side(kind, True, 0)
                side(kind, False, 1)
                to_sibling(kind, at(y_hi, 4)).start()

    def low_slots(hops):
        if hops in (0, 4):
            return [at(0, hops)]
        return [at(0, -hops), at(0, hops)]

    def from_cross(hops):
        for p in (0, 1):
            for k, slot in enumerate(low_slots(hops)):
                q = p if k == 0 else 1 - p
                arrived(kind_on, slot, q)
                to_pair(slot, q).start()
        for slot in low_slots(hops):
            to_sibling(kind_on, slot).start()

    def from_pair(hops):
        for slot in low_slots(hops):
            arrived(kind_swap, slot, 0)
            arrived(kind_swap, slot, 1)
            to_sibling(kind_swap, slot).start()


    def slot_at(steps, same):
        return ((x + steps + 4) % 4) * 2 + (y_lo if same else 1 - y_lo)

    def quarter(slot, q):
        return att.at[slot, pl.ds(q * QUARTER, QUARTER)]

    def send(slot, q, to_tp, sems):
        return pltpu.make_async_remote_copy(
            src_ref=quarter(slot, q), dst_ref=quarter(slot, q), send_sem=sems.at[slot, q],
            recv_sem=x_recv.at[slot, q], device_id=(ctx, to_tp), device_id_type=MESH,
        )

    x_to_right = lambda slot, q: send(slot, q, x_right, x_send_right)
    x_to_left = lambda slot, q: send(slot, q, x_left, x_send_left)
    x_to_pair = lambda slot, q: send(slot, q, pair, x_send_pair)

    def landed_at(slot, q):
        x_to_pair(slot, q).wait_recv()

    def edge_copy(k):
        to_ctx = above if k == 0 else below
        src = teacher_ref.at[pl.ds(TEACH - EDGE, EDGE)] if k == 0 else teacher_ref.at[pl.ds(0, EDGE)]
        dst = ext.at[pl.ds(0, EDGE)] if k == 0 else ext.at[pl.ds(EDGE + TEACH, EDGE)]
        return pltpu.make_async_remote_copy(
            src_ref=src, dst_ref=dst, send_sem=edge_send.at[k], recv_sem=edge_recv.at[k],
            device_id=(to_ctx, tp), device_id_type=MESH,
        )

    def grad_copy(k):
        return pltpu.make_async_remote_copy(
            src_ref=edges.at[k], dst_ref=landed.at[k], send_sem=edge_send.at[2 + k],
            recv_sem=edge_recv.at[2 + k], device_id=(above if k == 0 else below, tp),
            device_id_type=MESH,
        )

    def weight_load(slot):
        rows = pl.ds(pl.multiple_of(slot * DEPTH, DEPTH), DEPTH)
        return pltpu.make_async_copy(weight_ref.at[rows], weight.at[rows], load_weight.at[slot])

    student_load = pltpu.make_async_copy(student_ref, student, load.at[1])
    teacher_load = pltpu.make_async_copy(teacher_ref, ext.at[pl.ds(EDGE, TEACH)], load.at[2])
    def edge_and_loads():
        for k in range(2):
            edge_copy(k).start()
        student_load.start()
        teacher_load.start()
        order = [
            tp, pair, slot_at(-1, True), slot_at(1, True), slot_at(2, True),
            slot_at(-1, False), slot_at(1, False), slot_at(2, False),
        ]
        for slot in order:
            weight_load(slot).start()

    half_rows = 2 * S_DEV

    def score(block, c, masked=False):
        cols = slice(c * half_rows, (c + 1) * half_rows)
        keys = buf[0, pl.ds(pl.multiple_of(block * 2 * S_DEV, 2 * S_DEV), 2 * S_DEV), :]
        s = jnp.dot(keys, q_t[:, cols], preferred_element_type=jnp.float32)
        if masked:
            key_pos = lax.broadcasted_iota(jnp.int32, s.shape, 0)
            query_pos = lax.broadcasted_iota(jnp.int32, s.shape, 1) % S_DEV + core * S_DEV
            s = jnp.where(key_pos <= query_pos, s, LOW)
        scores[c] = s
        new_peak = jnp.max(s, axis=0, keepdims=True)
        if not masked:
            old = peak[:, cols]
            new_peak = jnp.maximum(old, new_peak)
            decay[:, cols] = jnp.exp2((old - new_peak) * EXP_SCALE)
        peak[:, cols] = new_peak

    def gather_values(block, c, first=False):
        cols = slice(c * half_rows, (c + 1) * half_rows)
        weights = jnp.exp2((scores[c] - peak[:, cols]) * EXP_SCALE)
        added = jnp.sum(weights, axis=0, keepdims=True)
        rounded = weights.astype(jnp.bfloat16)
        base = block * 2 * S_DEV
        product = None
        for k in range(2):
            parts = [
                buf[1, pl.ds(pl.multiple_of(base + k * S_DEV + g * HD, HD), HD), :]
                for g in range(2)
            ]
            values = jnp.concatenate(parts, axis=1)
            term = jnp.dot(
                values, rounded[k * S_DEV : (k + 1) * S_DEV], preferred_element_type=jnp.float32
            )
            product = term if product is None else product + term
        if first:
            total[:, cols] = added
            accum[:, cols] = product
        else:
            shrink = decay[:, cols]
            total[:, cols] = total[:, cols] * shrink + added
            accum[:, cols] = accum[:, cols] * shrink + product

    own_block = ctx // 2
    edge_and_loads()
    for kind in range(2):
        to_sibling(kind, sibling).wait_recv()
    score(own_block, 0, masked=True)
    score(own_block, 1, masked=True)
    gather_values(own_block, 0, first=True)
    total[:, half_rows:] = jnp.zeros((1, half_rows), jnp.float32)
    accum[:, half_rows:] = jnp.zeros((HD, half_rows), jnp.float32)
    decay[:, half_rows:] = jnp.ones((1, half_rows), jnp.float32)

    low_order = {2: (1, -1), 3: (1, 1), 4: (1, -2), 5: (1, 2), 7: (1, -3), 8: (1, 3), 9: (1, 4)}
    low_events = {
        1: [(ring, 1)], 2: [(from_pair, 1)], 3: [(ring, 2)], 4: [(from_pair, 2)], 5: [(ring, 3)],
        6: [(ring, 4)], 7: [(from_pair, 3)], 8: [(from_pair, 4)],
    }
    high_order = {
        1: (1, -1), 2: (1, 1), 3: (2, 0), 4: (1, -2), 5: (1, 2), 6: (2, -1), 7: (2, 1), 8: (1, -3),
        9: (1, 3), 10: (1, 4), 11: (2, -2), 12: (2, 2), 13: (2, -3), 14: (2, 3), 15: (2, 4),
    }
    high_events = {
        1: [(ring, 1), (from_cross, 0)], 2: [(ring, 2), (from_cross, 1), (from_pair, 0)],
        4: [(from_pair, 1)], 5: [(ring, 3), (from_cross, 2)], 7: [(from_pair, 2)],
        8: [(ring, 4), (from_cross, 3)], 10: [(from_pair, 3), (from_cross, 4)], 12: [(from_pair, 4)],
    }

    def lookup(n, field):
        low = pick(n, [low_order.get(k, (0, 0))[field] for k in range(16)])
        high = pick(n, [high_order.get(k, (0, 0))[field] for k in range(16)])
        return jnp.where(y_hi == 0, low, high)

    def step(n, before):
        plane = lookup(n, 0)
        block_z = (z + lookup(n, 1) + N_Z) % N_Z
        for hi, events, kinds in ((0, low_events, [y_lo]), (1, high_events, [0, 1])):
            @pl.when(y_hi == hi)
            def _(events=events, kinds=kinds):
                for k, todo in events.items():
                    @pl.when(n == k)
                    def _(todo=todo):
                        for action, hops in todo:
                            if action is ring:
                                ring(hops, kinds)
                            else:
                                action(hops)

        block = jnp.where(plane == 2, block_z, y_hi * N_Z + block_z)
        here = plane > 0

        @pl.when(here)
        def _():
            for kind in range(2):
                to_sibling(kind, block * 2 + 1 - core).wait_recv()

        def compute(prior):
            score(block, 0)
            gather_values(prior, 1)
            score(block, 1)
            gather_values(block, 0)
            return block

        return lax.cond(here & (block < own_block), compute, lambda prior: prior, before)

    last_block = lax.fori_loop(1, 16, step, own_block)
    gather_values(last_block, 1)
    for h in range(4):
        cols = slice(h * S_DEV, (h + 1) * S_DEV)
        att[tp, :, h * HD : (h + 1) * HD] = (accum[:, cols] / total[:, cols]).T.astype(jnp.bfloat16)


    for k in range(4):
        x_to_pair(tp, (2, 3, 0, 1)[k]).start()
        x_to_right(tp, (0, 2, 1, 3)[k]).start()
        x_to_left(tp, (1, 3, 0, 2)[k]).start()
    ext[WINDOW:, :] = jnp.zeros((ext.shape[0] - WINDOW, WIDTH), jnp.bfloat16)
    first = ctx * TEACH - EDGE
    start_row, len_row = start_ref[...], len_ref[...]
    row_pos = first + lax.broadcasted_iota(jnp.int32, (WINDOW, S_DEV), 0)
    inside = (row_pos >= start_row) & (row_pos < start_row + len_row)
    member_t[...] = jnp.where(inside, 1.0, 0.0).astype(jnp.bfloat16)
    wide_start = jnp.broadcast_to(start_row.astype(jnp.float32), (HD, S_DEV)).T[:, :1]
    wide_len = jnp.broadcast_to(len_row.astype(jnp.float32), (HD, S_DEV)).T
    counts[...] = 1.0 / wide_len
    col_pos = (first + lax.broadcasted_iota(jnp.int32, member.shape, 1)).astype(jnp.float32)
    inside = (col_pos >= wide_start) & (col_pos < wide_start + wide_len[:, :1])
    member[...] = jnp.where(inside, 1.0, 0.0).astype(jnp.bfloat16)
    student_load.wait()
    result[...] = student[...].astype(jnp.float32)

    def columns(j):
        return pl.ds(pl.multiple_of(j * TILE, TILE), TILE)

    def multiply(slot):
        weight_load(slot).wait()
        rows = pl.ds(pl.multiple_of(slot * DEPTH, DEPTH), DEPTH)

        @pl.loop(0, WIDTH // TILE)
        def _(j):
            result[:, columns(j)] += jnp.dot(
                att[slot], weight[rows, columns(j)], preferred_element_type=jnp.float32
            )

    prev, nxt = slot_at(-1, True), slot_at(1, True)
    far, far_other = slot_at(2, True), slot_at(2, False)
    prev_other, nxt_other = slot_at(-1, False), slot_at(1, False)

    landed_at(pair, 2)
    x_to_right(pair, 2).start()
    x_to_left(pair, 2).start()
    landed_at(pair, 3)
    x_to_left(pair, 3).start()
    x_to_right(pair, 3).start()
    multiply(tp)
    landed_at(prev, 0)
    x_to_right(prev, 0).start()
    x_to_pair(prev, 0).start()
    landed_at(nxt, 1)
    x_to_left(nxt, 1).start()
    x_to_pair(nxt, 1).start()
    landed_at(prev, 2)
    x_to_right(prev, 2).start()
    landed_at(nxt, 3)
    x_to_left(nxt, 3).start()
    landed_at(prev, 1)
    x_to_pair(prev, 1).start()
    landed_at(nxt, 0)
    x_to_pair(nxt, 0).start()
    teacher_load.wait()
    for k in range(2):
        edge_copy(k).wait_recv()

    @pl.loop(0, WIDTH // TILE)
    def _(j):
        summed = jnp.dot(member[...], ext[:, columns(j)], preferred_element_type=jnp.float32)
        target[:, columns(j)] = summed * counts[:, :1]

    landed_at(pair, 0)
    landed_at(pair, 1)
    landed_at(prev_other, 2)
    x_to_right(prev_other, 2).start()
    landed_at(nxt_other, 3)
    x_to_left(nxt_other, 3).start()
    multiply(pair)
    landed_at(far, 0)
    x_to_pair(far, 0).start()
    landed_at(far, 1)
    x_to_pair(far, 1).start()
    landed_at(prev, 3)
    multiply(prev)
    landed_at(nxt, 2)
    multiply(nxt)
    for q in (2, 3):
        landed_at(far, q)
    multiply(far)
    for q in (3, 0, 1):
        landed_at(prev_other, q)
    multiply(prev_other)
    for q in (2, 0, 1):
        landed_at(nxt_other, q)
    multiply(nxt_other)
    for q in (2, 3, 0, 1):
        landed_at(far_other, q)
    weight_load(far_other).wait()
    last_rows = pl.ds(pl.multiple_of(far_other * DEPTH, DEPTH), DEPTH)

    @pl.loop(0, WIDTH // TILE)
    def _(j):
        student32 = result[:, columns(j)] + jnp.dot(
            att[far_other], weight[last_rows, columns(j)], preferred_element_type=jnp.float32
        )
        out_ref[:, columns(j)] = student32.astype(jnp.bfloat16)
        weighted = ((student32 - target[:, columns(j)]) * counts[:, :1]).astype(jnp.bfloat16)
        spread = jnp.dot(member_t[...], weighted, preferred_element_type=jnp.float32)
        edges[0, :, columns(j)] = spread[EDGE + TEACH : EDGE + TEACH + HALO]
        edges[1, :, columns(j)] = spread[EDGE - HALO : EDGE]
        result[:, columns(j)] = spread[EDGE : EDGE + S_DEV]
        target[: TEACH - S_DEV, columns(j)] = spread[EDGE + S_DEV : EDGE + TEACH]

    for k in range(2):
        grad_copy(k).start()
    grad_ref[EDGE:S_DEV, :] = result[EDGE:, :].astype(jnp.bfloat16)
    rest = TEACH - S_DEV - EDGE
    grad_ref[S_DEV : TEACH - EDGE, :] = target[:rest, :].astype(jnp.bfloat16)
    for k in range(2):
        grad_copy(k).wait_recv()
    low = result[:EDGE, :] + jnp.concatenate([landed[0], jnp.zeros_like(landed[0])], axis=0)
    grad_ref[:EDGE, :] = low.astype(jnp.bfloat16)
    high = target[rest : rest + EDGE, :] + jnp.concatenate(
        [jnp.zeros_like(landed[1]), landed[1]], axis=0
    )
    grad_ref[TEACH - EDGE :, :] = high.astype(jnp.bfloat16)

    for k in range(2):
        edge_copy(k).wait_send()
        grad_copy(k).wait_send()
    for q in range(4):
        x_to_pair(tp, q).wait_send()
        x_to_right(tp, q).wait_send()
        x_to_left(tp, q).wait_send()
    for q in (2, 3):
        x_to_right(pair, q).wait_send()
        x_to_left(pair, q).wait_send()
    for slot, q in ((prev, 0), (prev, 2), (prev_other, 2)):
        x_to_right(slot, q).wait_send()
    for slot, q in ((nxt, 1), (nxt, 3), (nxt_other, 3)):
        x_to_left(slot, q).wait_send()
    for slot in (prev, nxt, far):
        for q in range(2):
            x_to_pair(slot, q).wait_send()
    def sent_own(kinds):
        for kind in kinds:
            for p in range(2):
                for hops in range(4 if p == 0 else 3):
                    to_right(kind, hops, p).wait_send()
                for hops in range(3 if p == 0 else 4):
                    to_left(kind, hops, p).wait_send()

    for_ring(sent_own)

    def sent(steps, _):
        slot = (z + steps) % N_Z * 2 + core
        for kind in range(2):
            to_sibling(kind, y_hi * 16 + slot).wait_send()

        @pl.when(y_hi == 0)
        def _():
            for p in range(2):
                to_cross(slot, p).wait_send()

        @pl.when((y_hi == 1) | (steps > 0))
        def _():
            for p in range(2):
                to_pair(slot, p).wait_send()

        @pl.when(y_hi == 1)
        def _():
            for kind in range(2):
                to_sibling(kind, slot).wait_send()

        return 0

    lax.fori_loop(0, N_Z, sent, 0)


def place_kernel(rows_ref, grad_in, out_ref, grad_ref, sems):
    copies = []
    for source, result, first in ((rows_ref, out_ref, 0), (grad_in, grad_ref, 4)):
        for k in range(4):
            size = source.shape[0] // 4
            part = pl.ds(k * size, size)
            copies.append(pltpu.make_async_copy(source.at[part], result.at[part], sems.at[first + k]))
    for one in copies:
        one.start()
    for one in copies:
        one.wait()


def body(student_rows, queries, keys_values, out_weight, teacher_rows, span_start, span_len):
    in_vmem, anywhere = pl.BlockSpec(memory_space=pltpu.VMEM), pl.BlockSpec(memory_space=pl.ANY)
    dma = pltpu.SemaphoreType.DMA
    bf16, f32 = jnp.bfloat16, jnp.float32
    wide = 4 * S_DEV
    results = (
        jax.ShapeDtypeStruct((S_DEV, WIDTH), bf16),
        jax.ShapeDtypeStruct((TEACH, WIDTH), bf16),
    )
    rows, grad = pl.pallas_call(
        layer_kernel,
        out_shape=results,
        in_specs=[anywhere] * 5 + [in_vmem] * 2,
        out_specs=(in_vmem, in_vmem),
        scratch_shapes=[
            pltpu.VMEM((2, 32 * S_DEV, HD), bf16),
            pltpu.VMEM((S_DEV, HD), bf16),
            pltpu.VMEM((S_DEV, DEPTH), bf16),
            pltpu.VMEM((HD, wide), bf16),
            pltpu.VMEM((2, 2 * S_DEV, wide // 2), f32),
            pltpu.VMEM((1, wide), f32),
            pltpu.VMEM((1, wide), f32),
            pltpu.VMEM((1, wide), f32),
            pltpu.VMEM((HD, wide), f32),
            pltpu.VMEM((8, S_DEV, DEPTH), bf16),
            pltpu.VMEM((8 * DEPTH, WIDTH), bf16),
            pltpu.VMEM((S_DEV, WIDTH), bf16),
            pltpu.VMEM((512, WIDTH), bf16),
            pltpu.VMEM((S_DEV, 512), bf16),
            pltpu.VMEM((WINDOW, S_DEV), bf16),
            pltpu.VMEM((S_DEV, WIDTH), f32),
            pltpu.VMEM((S_DEV, WIDTH), f32),
            pltpu.VMEM((S_DEV, HD), f32),
            pltpu.VMEM((2, HALO, WIDTH), f32),
            pltpu.VMEM((2, HALO, WIDTH), f32),
            dma((2, 64)), dma((2, 32)), dma((2, 8)), dma((2, 8)), dma((2, 32)), dma((16,)), dma((16,)),
            dma((8, 4)), dma((8, 4)), dma((8, 4)), dma((8, 4)), dma((5,)), dma((8,)), dma((4,)), dma((4,)),
        ],
        compiler_params=pltpu.CompilerParams(
            collective_id=0, has_side_effects=True, vmem_limit_bytes=60 << 20
        ),
        name="layer",
    )(
        queries, keys_values, student_rows, out_weight, teacher_rows,
        span_start.reshape(1, S_DEV), span_len.reshape(1, S_DEV),
    )
    return pl.pallas_call(
        place_kernel,
        out_shape=results,
        in_specs=[anywhere] * 2,
        out_specs=(anywhere, anywhere),
        scratch_shapes=[dma((8,))],
        compiler_params=pltpu.CompilerParams(vmem_limit_bytes=60 << 20),
        name="place",
    )(rows, grad)


def solution(mesh):
    return jax.shard_map(
        body,
        mesh=mesh,
        in_specs=(
            P("ctx", "tp"),
            P("ctx", "tp"),
            P(None, "ctx", None),
            P(None, "tp"),
            P("ctx", "tp"),
            P("ctx"),
            P("ctx"),
        ),
        out_specs=(P("ctx", "tp"), P("ctx", "tp")),
        check_vma=False,
    )
```

```python
import functools
import math

import jax
import jax.numpy as jnp
from jax import lax
from jax.experimental import pallas as pl
from jax.experimental.pallas import tpu as pltpu
from jax.sharding import PartitionSpec as P

HD = 128
S_DEV = 256
HALO = 8
N_Z = 8
MESH = pl.DeviceIdType.MESH
EXP_SCALE = math.log2(math.e) / math.sqrt(HD)
LOW = -1e30

TEACH = 384
EDGE = 16
WINDOW = TEACH + 2 * EDGE
DEPTH = 512
WIDTH = 1024
QUARTER = S_DEV // 4
TILE = 256


def pick(step, table):
    value = table[0]
    for k in range(1, len(table)):
        value = jnp.where(step == k, table[k], value)
    return value


def layer_kernel(
    q_ref, kv_ref, student_ref, weight_ref, teacher_ref, start_ref, len_ref, out_ref, grad_ref,
    buf, own_v, q_rows, q_t, scores, peak, decay, total, accum,
    att, weight, student, ext, member, member_t, result, target, counts, edges, landed,
    starts, lens, recv, recv_sib, sent, x_recv, load, edge_recv,
):
    ctx, tp = lax.axis_index("ctx"), lax.axis_index("tp")
    core, z, y_hi = ctx % 2, (ctx // 2) % N_Z, ctx // 16
    x, y_lo = tp // 2, tp % 2
    sibling = ctx + 1 - 2 * core
    right = y_hi * 16 + ((z + 1) % N_Z) * 2 + core
    left = y_hi * 16 + ((z + N_Z - 1) % N_Z) * 2 + core
    other_hi = (ctx + 16) % 32
    pair = tp + 1 - 2 * y_lo
    kind_on = jnp.where(y_hi == 0, y_lo, 1 - y_lo)
    kind_swap = 1 - kind_on
    x_right, x_left = ((x + 1) % 4) * 2 + y_lo, ((x + 3) % 4) * 2 + y_lo
    above, below = (ctx + 1) % 32, (ctx + 31) % 32

    def at(hi, steps):
        return hi * 16 + ((z + steps + N_Z) % N_Z) * 2 + core

    def piece(kind, slot, p):
        return buf.at[kind, pl.ds(pl.multiple_of(slot * S_DEV + p * HD, HD), HD)]

    def part(kind, slot):
        return buf.at[kind, pl.ds(pl.multiple_of(slot * S_DEV, S_DEV), S_DEV)]

    def copy(kind, slot, p, to_ctx, to_tp):
        return pltpu.make_async_remote_copy(
            src_ref=piece(kind, slot, p), dst_ref=piece(kind, slot, p), send_sem=sent.at[0],
            recv_sem=recv.at[kind, slot // 2 * 2 + p], device_id=(to_ctx, to_tp), device_id_type=MESH,
        )

    def arrived(kind, slot, p):
        copy(kind, slot, p, ctx, pair).wait_recv()

    def to_sibling(kind, slot):
        return pltpu.make_async_remote_copy(
            src_ref=part(kind, slot), dst_ref=part(kind, slot), send_sem=sent.at[0],
            recv_sem=recv_sib.at[slot // 2], device_id=(sibling, tp), device_id_type=MESH,
        )

    def from_sibling(block):
        both = buf.at[0, pl.ds(0, 2 * S_DEV)]
        pltpu.make_async_remote_copy(
            src_ref=both, dst_ref=both, send_sem=sent.at[0], recv_sem=recv_sib.at[block],
            device_id=(sibling, tp), device_id_type=MESH,
        ).wait_recv()

    def to_right(kind, hops, p):
        return copy(kind, at(y_hi, -hops), p, right, tp)

    def to_left(kind, hops, p):
        return copy(kind, at(y_hi, hops), p, left, tp)

    def to_cross(slot, p):
        return copy(y_lo, slot, p, other_hi, pair)

    def to_pair(slot, p):
        return copy(kind_on, slot, p, ctx, pair)

    k_load = pltpu.make_async_copy(
        kv_ref.at[0, :, pl.ds(pl.multiple_of(x * HD, HD), HD)], part(0, ctx), load.at[3]
    )
    v_load = pltpu.make_async_copy(
        kv_ref.at[1, :, pl.ds(pl.multiple_of(x * HD, HD), HD)], own_v, load.at[0]
    )
    q_load = pltpu.make_async_copy(q_ref, q_rows, load.at[4])
    start_load = pltpu.make_async_copy(start_ref, starts, load.at[6])
    len_load = pltpu.make_async_copy(len_ref, lens, load.at[7])
    v_load.start()
    k_load.start()
    q_load.start()
    start_load.start()
    len_load.start()
    barrier = pltpu.get_barrier_semaphore()
    for to_ctx, to_tp in (
        (right, tp), (left, tp), (sibling, tp), (other_hi, pair), (ctx, pair),
        (ctx, x_right), (ctx, x_left), (above, tp), (below, tp),
    ):
        pl.semaphore_signal(barrier, inc=1, device_id=(to_ctx, to_tp), device_id_type=MESH)
    v_load.wait()
    v_own = own_v[...].astype(jnp.float32)
    for half in range(2):
        turned = v_own[half * HD : (half + 1) * HD].T.astype(jnp.bfloat16)
        start = pl.multiple_of(ctx * S_DEV + half * HD, HD)
        buf[1, pl.ds(start, HD), :] = turned
    q_load.wait()
    for h in range(4):
        q_t[:, h * S_DEV : (h + 1) * S_DEV] = (
            q_rows[:, h * HD : (h + 1) * HD].astype(jnp.float32).T.astype(jnp.bfloat16)
        )
    k_load.wait()
    pl.semaphore_wait(barrier, 9)

    def for_ring(action):
        @pl.when(y_hi == 0)
        def _():
            action([y_lo])

        @pl.when(y_hi == 1)
        def _():
            action([0, 1])

    def start_own(kinds):
        for p in range(2):
            for kind in kinds:
                to_right(kind, 0, p).start()
                to_left(kind, 0, 1 - p).start()
            if len(kinds) == 1:
                to_cross(ctx, p).start()

    for_ring(start_own)
    for kind in range(2):
        to_sibling(kind, ctx).start()

    def ring(hops, kinds):
        def side(kind, moving_right, p):
            slot = at(y_hi, -hops if moving_right else hops)
            arrived(kind, slot, p)
            last = 3 if (p == 0) == moving_right else 2
            if hops <= last:
                (to_right if moving_right else to_left)(kind, hops, p).start()
            if len(kinds) == 1:
                to_cross(slot, p).start()
                to_pair(slot, p).start()

        if hops < 4:
            for k in range(2):
                for kind in kinds:
                    side(kind, True, k)
                    side(kind, False, 1 - k)
            for kind in kinds:
                to_sibling(kind, at(y_hi, -hops)).start()
                to_sibling(kind, at(y_hi, hops)).start()
        else:
            for kind in kinds:
                side(kind, True, 0)
                side(kind, False, 1)
                to_sibling(kind, at(y_hi, 4)).start()

    def low_slots(hops):
        if hops in (0, 4):
            return [at(0, hops)]
        return [at(0, -hops), at(0, hops)]

    def from_cross(hops):
        for p in (0, 1):
            for k, slot in enumerate(low_slots(hops)):
                q = p if k == 0 else 1 - p
                arrived(kind_on, slot, q)
                to_pair(slot, q).start()
        for slot in low_slots(hops):
            to_sibling(kind_on, slot).start()

    def from_pair(hops):
        for slot in low_slots(hops):
            arrived(kind_swap, slot, 0)
            arrived(kind_swap, slot, 1)
            to_sibling(kind_swap, slot).start()


    def slot_at(steps, same):
        return ((x + steps + 4) % 4) * 2 + (y_lo if same else 1 - y_lo)

    def quarter(slot, q):
        return att.at[slot, pl.ds(q * QUARTER, QUARTER)]

    def send(slot, q, to_tp):
        return pltpu.make_async_remote_copy(
            src_ref=quarter(slot, q), dst_ref=quarter(slot, q), send_sem=sent.at[0],
            recv_sem=x_recv.at[slot, q], device_id=(ctx, to_tp), device_id_type=MESH,
        )

    x_to_right = lambda slot, q: send(slot, q, x_right)
    x_to_left = lambda slot, q: send(slot, q, x_left)
    x_to_pair = lambda slot, q: send(slot, q, pair)

    def landed_at(slot, q):
        x_to_pair(slot, q).wait_recv()

    def edge_copy(k):
        to_ctx = above if k == 0 else below
        src = teacher_ref.at[pl.ds(TEACH - EDGE, EDGE)] if k == 0 else teacher_ref.at[pl.ds(0, EDGE)]
        dst = ext.at[pl.ds(0, EDGE)] if k == 0 else ext.at[pl.ds(EDGE + TEACH, EDGE)]
        return pltpu.make_async_remote_copy(
            src_ref=src, dst_ref=dst, send_sem=sent.at[0], recv_sem=edge_recv.at[k],
            device_id=(to_ctx, tp), device_id_type=MESH,
        )

    def grad_copy(k):
        return pltpu.make_async_remote_copy(
            src_ref=edges.at[k], dst_ref=landed.at[k], send_sem=sent.at[0],
            recv_sem=edge_recv.at[2 + k], device_id=(above if k == 0 else below, tp),
            device_id_type=MESH,
        )

    def weight_load(slot):
        rows = pl.ds(pl.multiple_of(slot * DEPTH, DEPTH), DEPTH)
        return pltpu.make_async_copy(weight_ref.at[rows], weight.at[rows], load.at[5])

    student_load = pltpu.make_async_copy(student_ref, student, load.at[1])
    teacher_load = pltpu.make_async_copy(teacher_ref, ext.at[pl.ds(EDGE, TEACH)], load.at[2])
    def edge_and_loads():
        for k in range(2):
            edge_copy(k).start()
        student_load.start()
        teacher_load.start()
        for slot in range(8):
            weight_load(slot).start()

    half_rows = 2 * S_DEV

    def score(block, c, masked=False):
        cols = slice(c * half_rows, (c + 1) * half_rows)
        keys = buf[0, pl.ds(pl.multiple_of(block * 2 * S_DEV, 2 * S_DEV), 2 * S_DEV), :]
        s = jnp.dot(keys, q_t[:, cols], preferred_element_type=jnp.float32)
        if masked:
            key_pos = lax.broadcasted_iota(jnp.int32, s.shape, 0)
            query_pos = lax.broadcasted_iota(jnp.int32, s.shape, 1) % S_DEV + core * S_DEV
            s = jnp.where(key_pos <= query_pos, s, LOW)
        scores[c] = s
        new_peak = jnp.max(s, axis=0, keepdims=True)
        if not masked:
            old = peak[:, cols]
            new_peak = jnp.maximum(old, new_peak)
            decay[:, cols] = jnp.exp2((old - new_peak) * EXP_SCALE)
        peak[:, cols] = new_peak

    def gather_values(block, c, first=False):
        cols = slice(c * half_rows, (c + 1) * half_rows)
        weights = jnp.exp2((scores[c] - peak[:, cols]) * EXP_SCALE)
        added = jnp.sum(weights, axis=0, keepdims=True)
        rounded = weights.astype(jnp.bfloat16)
        base = block * 2 * S_DEV
        product = None
        for k in range(2):
            parts = [
                buf[1, pl.ds(pl.multiple_of(base + k * S_DEV + g * HD, HD), HD), :]
                for g in range(2)
            ]
            values = jnp.concatenate(parts, axis=1)
            term = jnp.dot(
                values, rounded[k * S_DEV : (k + 1) * S_DEV], preferred_element_type=jnp.float32
            )
            product = term if product is None else product + term
        if first:
            total[:, cols] = added
            accum[:, cols] = product
        else:
            shrink = decay[:, cols]
            total[:, cols] = total[:, cols] * shrink + added
            accum[:, cols] = accum[:, cols] * shrink + product

    own_block = ctx // 2
    from_sibling(ctx // 2)
    score(own_block, 0, masked=True)
    score(own_block, 1, masked=True)
    gather_values(own_block, 0, first=True)
    total[:, half_rows:] = jnp.zeros((1, half_rows), jnp.float32)
    accum[:, half_rows:] = jnp.zeros((HD, half_rows), jnp.float32)
    decay[:, half_rows:] = jnp.ones((1, half_rows), jnp.float32)

    low_order = {2: (1, -1), 3: (1, 1), 4: (1, -2), 5: (1, 2), 7: (1, -3), 8: (1, 3), 9: (1, 4)}
    low_events = {
        1: [(ring, 1)], 2: [(from_pair, 1)], 3: [(ring, 2)], 4: [(from_pair, 2)], 5: [(ring, 3)],
        6: [(ring, 4)], 7: [(from_pair, 3)], 8: [(from_pair, 4)],
    }
    high_order = {
        1: (1, -1), 2: (1, 1), 3: (2, 0), 4: (1, -2), 5: (1, 2), 6: (2, -1), 7: (2, 1), 8: (1, -3),
        9: (1, 3), 10: (1, 4), 11: (2, -2), 12: (2, 2), 13: (2, -3), 14: (2, 3), 15: (2, 4),
    }
    high_events = {
        1: [(ring, 1), (from_cross, 0)], 2: [(ring, 2), (from_cross, 1), (from_pair, 0)],
        4: [(from_pair, 1)], 5: [(ring, 3), (from_cross, 2)], 7: [(from_pair, 2)],
        8: [(ring, 4), (from_cross, 3)], 10: [(from_pair, 3), (from_cross, 4)], 12: [(from_pair, 4)],
    }

    def lookup(n, field):
        low = pick(n, [low_order.get(k, (0, 0))[field] for k in range(16)])
        high = pick(n, [high_order.get(k, (0, 0))[field] for k in range(16)])
        return jnp.where(y_hi == 0, low, high)

    def step(n, before):
        plane = lookup(n, 0)
        block_z = (z + lookup(n, 1) + N_Z) % N_Z
        for hi, events, kinds in ((0, low_events, [y_lo]), (1, high_events, [0, 1])):
            @pl.when(y_hi == hi)
            def _(events=events, kinds=kinds):
                for k, todo in events.items():
                    @pl.when(n == k)
                    def _(todo=todo):
                        for action, hops in todo:
                            if action is ring:
                                ring(hops, kinds)
                            else:
                                action(hops)

        @pl.when(n == 9)
        def _():
            edge_and_loads()

        block = jnp.where(plane == 2, block_z, y_hi * N_Z + block_z)
        here = plane > 0

        @pl.when(here)
        def _():
            from_sibling(block)

        def compute(prior):
            score(block, 0)
            gather_values(prior, 1)
            score(block, 1)
            gather_values(block, 0)
            return block

        return lax.cond(here & (block < own_block), compute, lambda prior: prior, before)

    last_block = lax.fori_loop(1, 16, step, own_block)
    gather_values(last_block, 1)
    for h in range(4):
        cols = slice(h * S_DEV, (h + 1) * S_DEV)
        att[tp, :, h * HD : (h + 1) * HD] = (accum[:, cols] / total[:, cols]).T.astype(jnp.bfloat16)


    for k in range(4):
        x_to_pair(tp, (2, 3, 0, 1)[k]).start()
        x_to_right(tp, (0, 2, 1, 3)[k]).start()
        x_to_left(tp, (1, 3, 0, 2)[k]).start()
    ext[WINDOW:, :] = jnp.zeros((ext.shape[0] - WINDOW, WIDTH), jnp.bfloat16)
    first = ctx * TEACH - EDGE
    start_load.wait()
    len_load.wait()
    start_row, len_row = starts[...], lens[...]
    row_pos = first + lax.broadcasted_iota(jnp.int32, (WINDOW, S_DEV), 0)
    inside = (row_pos >= start_row) & (row_pos < start_row + len_row)
    member_t[...] = jnp.where(inside, 1.0, 0.0).astype(jnp.bfloat16)
    wide_start = jnp.broadcast_to(start_row.astype(jnp.float32), (HD, S_DEV)).T[:, :1]
    wide_len = jnp.broadcast_to(len_row.astype(jnp.float32), (HD, S_DEV)).T
    counts[...] = 1.0 / wide_len
    col_pos = (first + lax.broadcasted_iota(jnp.int32, member.shape, 1)).astype(jnp.float32)
    inside = (col_pos >= wide_start) & (col_pos < wide_start + wide_len[:, :1])
    member[...] = jnp.where(inside, 1.0, 0.0).astype(jnp.bfloat16)
    student_load.wait()
    result[...] = student[...].astype(jnp.float32)

    def columns(j):
        return pl.ds(pl.multiple_of(j * TILE, TILE), TILE)

    def multiply(slot):
        rows = pl.ds(pl.multiple_of(slot * DEPTH, DEPTH), DEPTH)

        @pl.loop(0, WIDTH // TILE)
        def _(j):
            result[:, columns(j)] += jnp.dot(
                att[slot], weight[rows, columns(j)], preferred_element_type=jnp.float32
            )

    prev, nxt = slot_at(-1, True), slot_at(1, True)
    far, far_other = slot_at(2, True), slot_at(2, False)
    prev_other, nxt_other = slot_at(-1, False), slot_at(1, False)

    landed_at(pair, 2)
    x_to_right(pair, 2).start()
    x_to_left(pair, 2).start()
    landed_at(pair, 3)
    x_to_left(pair, 3).start()
    x_to_right(pair, 3).start()
    pltpu.make_async_copy(weight_ref, weight, load.at[5]).wait()
    multiply(tp)
    landed_at(prev, 0)
    x_to_right(prev, 0).start()
    x_to_pair(prev, 0).start()
    landed_at(nxt, 1)
    x_to_left(nxt, 1).start()
    x_to_pair(nxt, 1).start()
    landed_at(prev, 2)
    x_to_right(prev, 2).start()
    landed_at(nxt, 3)
    x_to_left(nxt, 3).start()
    landed_at(prev, 1)
    x_to_pair(prev, 1).start()
    landed_at(nxt, 0)
    x_to_pair(nxt, 0).start()
    teacher_load.wait()
    for k in range(2):
        edge_copy(k).wait_recv()

    @pl.loop(0, WIDTH // TILE)
    def _(j):
        summed = jnp.dot(member[...], ext[:, columns(j)], preferred_element_type=jnp.float32)
        target[:, columns(j)] = summed * counts[:, :1]

    landed_at(pair, 0)
    landed_at(pair, 1)
    landed_at(prev_other, 2)
    x_to_right(prev_other, 2).start()
    landed_at(nxt_other, 3)
    x_to_left(nxt_other, 3).start()
    multiply(pair)
    landed_at(far, 0)
    x_to_pair(far, 0).start()
    landed_at(far, 1)
    x_to_pair(far, 1).start()
    landed_at(prev, 3)
    multiply(prev)
    landed_at(nxt, 2)
    multiply(nxt)
    for q in (2, 3):
        landed_at(far, q)
    multiply(far)
    for q in (3, 0, 1):
        landed_at(prev_other, q)
    multiply(prev_other)
    for q in (2, 0, 1):
        landed_at(nxt_other, q)
    multiply(nxt_other)
    for q in (2, 3, 0, 1):
        landed_at(far_other, q)
    last_rows = pl.ds(pl.multiple_of(far_other * DEPTH, DEPTH), DEPTH)

    @pl.loop(0, WIDTH // TILE)
    def _(j):
        student32 = result[:, columns(j)] + jnp.dot(
            att[far_other], weight[last_rows, columns(j)], preferred_element_type=jnp.float32
        )
        student[:, columns(j)] = student32.astype(jnp.bfloat16)
        weighted = ((student32 - target[:, columns(j)]) * counts[:, :1]).astype(jnp.bfloat16)
        spread = jnp.dot(member_t[...], weighted, preferred_element_type=jnp.float32)
        edges[0, :, columns(j)] = spread[EDGE + TEACH : EDGE + TEACH + HALO]
        edges[1, :, columns(j)] = spread[EDGE - HALO : EDGE]
        result[:, columns(j)] = spread[EDGE : EDGE + S_DEV]
        target[: TEACH - S_DEV, columns(j)] = spread[EDGE + S_DEV : EDGE + TEACH]

    for k in range(2):
        grad_copy(k).start()
    out_store = pltpu.make_async_copy(student, out_ref, load.at[0])
    out_store.start()
    ext[EDGE:S_DEV, :] = result[EDGE:, :].astype(jnp.bfloat16)
    rest = TEACH - S_DEV - EDGE
    ext[S_DEV : TEACH - EDGE, :] = target[:rest, :].astype(jnp.bfloat16)
    grad_stores = [
        pltpu.make_async_copy(ext.at[part], grad_ref.at[part], load.at[1 + k])
        for k, part in enumerate(
            (pl.ds(EDGE, TEACH - 2 * EDGE), pl.ds(0, EDGE), pl.ds(TEACH - EDGE, EDGE))
        )
    ]
    grad_stores[0].start()
    for k in range(2):
        grad_copy(k).wait_recv()
    low = result[:EDGE, :] + jnp.concatenate([landed[0], jnp.zeros_like(landed[0])], axis=0)
    ext[:EDGE, :] = low.astype(jnp.bfloat16)
    grad_stores[1].start()
    high = target[rest : rest + EDGE, :] + jnp.concatenate(
        [jnp.zeros_like(landed[1]), landed[1]], axis=0
    )
    ext[TEACH - EDGE : TEACH, :] = high.astype(jnp.bfloat16)
    grad_stores[2].start()

    out_store.wait()
    for store in grad_stores:
        store.wait()

    def all_sent(pieces):
        rows = weight.at[pl.ds(0, pieces * 16)]
        pltpu.make_async_remote_copy(
            src_ref=rows, dst_ref=rows, send_sem=sent.at[0], recv_sem=edge_recv.at[0],
            device_id=(sibling, tp), device_id_type=MESH,
        ).wait_send()

    @pl.when(y_hi == 0)
    def _():
        all_sent(14 + 16 + 14 + 32 + 60)

    @pl.when(y_hi == 1)
    def _():
        all_sent(28 + 16 + 64 + 60)


def place_kernel(rows_in, grad_in, out_ref, grad_ref, rows, grad, sems):
    pairs = []
    for source, middle, result in ((rows_in, rows, out_ref), (grad_in, grad, grad_ref)):
        for k in range(2):
            size = source.shape[0] // 2
            part = pl.ds(k * size, size)
            at = len(pairs)
            pairs.append((
                pltpu.make_async_copy(source.at[part], middle.at[part], sems.at[0, at]),
                pltpu.make_async_copy(middle.at[part], result.at[part], sems.at[1, at]),
            ))
    for fetch, _ in pairs:
        fetch.start()
    for fetch, store in pairs:
        fetch.wait()
        store.start()
    for _, store in pairs:
        store.wait()


def body(student_rows, queries, keys_values, out_weight, teacher_rows, span_start, span_len):
    anywhere = pl.BlockSpec(memory_space=pl.ANY)
    dma = pltpu.SemaphoreType.DMA
    bf16, f32 = jnp.bfloat16, jnp.float32
    wide = 4 * S_DEV
    results = (
        jax.ShapeDtypeStruct((S_DEV, WIDTH), bf16),
        jax.ShapeDtypeStruct((TEACH, WIDTH), bf16),
    )
    rows, grad = pl.pallas_call(
        layer_kernel,
        out_shape=results,
        in_specs=[anywhere] * 7,
        out_specs=(anywhere, anywhere),
        scratch_shapes=[
            pltpu.VMEM((2, 32 * S_DEV, HD), bf16),
            pltpu.VMEM((S_DEV, HD), bf16),
            pltpu.VMEM((S_DEV, DEPTH), bf16),
            pltpu.VMEM((HD, wide), bf16),
            pltpu.VMEM((2, 2 * S_DEV, wide // 2), f32),
            pltpu.VMEM((1, wide), f32),
            pltpu.VMEM((1, wide), f32),
            pltpu.VMEM((1, wide), f32),
            pltpu.VMEM((HD, wide), f32),
            pltpu.VMEM((8, S_DEV, DEPTH), bf16),
            pltpu.VMEM((8 * DEPTH, WIDTH), bf16),
            pltpu.VMEM((S_DEV, WIDTH), bf16),
            pltpu.VMEM((512, WIDTH), bf16),
            pltpu.VMEM((S_DEV, 512), bf16),
            pltpu.VMEM((WINDOW, S_DEV), bf16),
            pltpu.VMEM((S_DEV, WIDTH), f32),
            pltpu.VMEM((S_DEV, WIDTH), f32),
            pltpu.VMEM((S_DEV, HD), f32),
            pltpu.VMEM((2, HALO, WIDTH), f32),
            pltpu.VMEM((2, HALO, WIDTH), f32),
            pltpu.VMEM((1, S_DEV), jnp.int32),
            pltpu.VMEM((1, S_DEV), jnp.int32),
            dma((2, 32)), dma((16,)), dma((1,)), dma((8, 4)), dma((8,)), dma((4,)),
        ],
        compiler_params=pltpu.CompilerParams(
            collective_id=0, has_side_effects=True, vmem_limit_bytes=60 << 20
        ),
        name="layer",
    )(
        queries, keys_values, student_rows, out_weight, teacher_rows,
        span_start.reshape(1, S_DEV), span_len.reshape(1, S_DEV),
    )
    return pl.pallas_call(
        place_kernel,
        out_shape=results,
        in_specs=[anywhere] * 2,
        out_specs=(anywhere, anywhere),
        scratch_shapes=[
            pltpu.VMEM((S_DEV, WIDTH), bf16),
            pltpu.VMEM((TEACH, WIDTH), bf16),
            dma((2, 4)),
        ],
        compiler_params=pltpu.CompilerParams(vmem_limit_bytes=60 << 20),
        name="place",
    )(rows, grad)


def solution(mesh):
    return jax.shard_map(
        body,
        mesh=mesh,
        in_specs=(
            P("ctx", "tp"),
            P("ctx", "tp"),
            P(None, "ctx", None),
            P(None, "tp"),
            P("ctx", "tp"),
            P("ctx"),
            P("ctx"),
        ),
        out_specs=(P("ctx", "tp"), P("ctx", "tp")),
        check_vma=False,
    )
```

```python
import functools
import math

import jax
import jax.numpy as jnp
from jax import lax
from jax.experimental import pallas as pl
from jax.experimental.pallas import tpu as pltpu
from jax.sharding import PartitionSpec as P

HD = 128
S_DEV = 256
HALO = 8
N_Z = 8
MESH = pl.DeviceIdType.MESH
EXP_SCALE = math.log2(math.e) / math.sqrt(HD)
LOW = -1e30

TEACH = 384
EDGE = 16
WINDOW = TEACH + 2 * EDGE
DEPTH = 512
WIDTH = 1024
QUARTER = S_DEV // 4
TILE = 256


def pick(step, table):
    value = table[0]
    for k in range(1, len(table)):
        value = jnp.where(step == k, table[k], value)
    return value


def layer_kernel(
    q_ref, kv_ref, student_ref, weight_ref, teacher_ref, start_ref, len_ref, out_ref, grad_ref,
    buf, own_v, q_rows, q_t, scores, peak, decay, total, accum,
    att, weight, student, ext, member, member_t, result, target, counts, edges, landed,
    starts, lens, recv, recv_sib, sent, x_recv, load, edge_recv,
):
    ctx, tp = lax.axis_index("ctx"), lax.axis_index("tp")
    core, z, y_hi = ctx % 2, (ctx // 2) % N_Z, ctx // 16
    x, y_lo = tp // 2, tp % 2
    sibling = ctx + 1 - 2 * core
    right = y_hi * 16 + ((z + 1) % N_Z) * 2 + core
    left = y_hi * 16 + ((z + N_Z - 1) % N_Z) * 2 + core
    other_hi = (ctx + 16) % 32
    pair = tp + 1 - 2 * y_lo
    kind_on = jnp.where(y_hi == 0, y_lo, 1 - y_lo)
    kind_swap = 1 - kind_on
    x_right, x_left = ((x + 1) % 4) * 2 + y_lo, ((x + 3) % 4) * 2 + y_lo
    x_far = ((x + 2) % 4) * 2 + y_lo
    above, below = (ctx + 1) % 32, (ctx + 31) % 32

    def at(hi, steps):
        return hi * 16 + ((z + steps + N_Z) % N_Z) * 2 + core

    def piece(kind, slot, p):
        return buf.at[kind, pl.ds(pl.multiple_of(slot * S_DEV + p * HD, HD), HD)]

    def part(kind, slot):
        return buf.at[kind, pl.ds(pl.multiple_of(slot * S_DEV, S_DEV), S_DEV)]

    def copy(kind, slot, p, to_ctx, to_tp):
        return pltpu.make_async_remote_copy(
            src_ref=piece(kind, slot, p), dst_ref=piece(kind, slot, p), send_sem=sent.at[0],
            recv_sem=recv.at[kind, slot // 2 * 2 + p], device_id=(to_ctx, to_tp), device_id_type=MESH,
        )

    def arrived(kind, slot, p):
        copy(kind, slot, p, ctx, pair).wait_recv()

    def to_sibling(kind, slot):
        return pltpu.make_async_remote_copy(
            src_ref=part(kind, slot), dst_ref=part(kind, slot), send_sem=sent.at[0],
            recv_sem=recv_sib.at[slot // 2], device_id=(sibling, tp), device_id_type=MESH,
        )

    def from_sibling(block):
        both = buf.at[0, pl.ds(0, 2 * S_DEV)]
        pltpu.make_async_remote_copy(
            src_ref=both, dst_ref=both, send_sem=sent.at[0], recv_sem=recv_sib.at[block],
            device_id=(sibling, tp), device_id_type=MESH,
        ).wait_recv()

    def to_right(kind, hops, p):
        return copy(kind, at(y_hi, -hops), p, right, tp)

    def to_left(kind, hops, p):
        return copy(kind, at(y_hi, hops), p, left, tp)

    def to_second(slot, p, steps):
        return copy(y_lo, slot, p, at(y_hi, steps), tp)

    def to_cross(slot, p):
        return copy(y_lo, slot, p, other_hi, pair)

    def to_pair(slot, p):
        return copy(kind_on, slot, p, ctx, pair)

    k_load = pltpu.make_async_copy(
        kv_ref.at[0, :, pl.ds(pl.multiple_of(x * HD, HD), HD)], part(0, ctx), load.at[3]
    )
    v_load = pltpu.make_async_copy(
        kv_ref.at[1, :, pl.ds(pl.multiple_of(x * HD, HD), HD)], own_v, load.at[0]
    )
    q_load = pltpu.make_async_copy(q_ref, q_rows, load.at[4])
    start_load = pltpu.make_async_copy(start_ref, starts, load.at[6])
    len_load = pltpu.make_async_copy(len_ref, lens, load.at[7])
    v_load.start()
    k_load.start()
    q_load.start()
    start_load.start()
    len_load.start()
    barrier = pltpu.get_barrier_semaphore()
    for to_ctx, to_tp in (
        (right, tp), (left, tp), (sibling, tp), (other_hi, pair), (ctx, pair),
        (ctx, x_right), (ctx, x_left), (ctx, x_far), (above, tp), (below, tp),
        (at(y_hi, 2), tp), (at(y_hi, -2), tp),
    ):
        pl.semaphore_signal(barrier, inc=1, device_id=(to_ctx, to_tp), device_id_type=MESH)
    v_load.wait()
    v_own = own_v[...].astype(jnp.float32)
    for half in range(2):
        turned = v_own[half * HD : (half + 1) * HD].T.astype(jnp.bfloat16)
        start = pl.multiple_of(ctx * S_DEV + half * HD, HD)
        buf[1, pl.ds(start, HD), :] = turned
    q_load.wait()
    for h in range(4):
        q_t[:, h * S_DEV : (h + 1) * S_DEV] = (
            q_rows[:, h * HD : (h + 1) * HD].astype(jnp.float32).T.astype(jnp.bfloat16)
        )
    k_load.wait()
    pl.semaphore_wait(barrier, 12)

    def for_ring(action):
        @pl.when(y_hi == 0)
        def _():
            action([y_lo])

        @pl.when(y_hi == 1)
        def _():
            action([0, 1])

    def start_own(kinds):
        if len(kinds) == 1:
            for p in range(2):
                to_second(ctx, p, 2).start()
                to_second(ctx, 1 - p, -2).start()
                to_cross(ctx, p).start()
        for p in range(2):
            for kind in kinds:
                to_right(kind, 0, p).start()
                to_left(kind, 0, 1 - p).start()

    for_ring(start_own)
    for kind in range(2):
        to_sibling(kind, ctx).start()

    def low_ring(hops):
        def side(sign, p):
            slot = at(0, sign * hops)
            arrived(y_lo, slot, p)
            if hops == 2:
                copy(y_lo, slot, p, left if sign > 0 else right, tp).start()
                if (p == 0) == (sign < 0):
                    to_second(slot, p, -2 * sign).start()
            to_cross(slot, p).start()
            to_pair(slot, p).start()

        for p in range(2):
            side(-1, p)
            if hops < 4:
                side(1, 1 - p)
        for slot in low_slots(hops):
            to_sibling(y_lo, slot).start()

    def ring(hops):
        def side(kind, moving_right, p):
            arrived(kind, at(y_hi, -hops if moving_right else hops), p)
            last = 3 if (p == 0) == moving_right else 2
            if hops <= last:
                (to_right if moving_right else to_left)(kind, hops, p).start()

        kinds = range(2)
        if hops < 4:
            for k in range(2):
                for kind in kinds:
                    side(kind, True, k)
                    side(kind, False, 1 - k)
            for kind in kinds:
                to_sibling(kind, at(y_hi, -hops)).start()
                to_sibling(kind, at(y_hi, hops)).start()
        else:
            for kind in kinds:
                side(kind, True, 0)
                side(kind, False, 1)
                to_sibling(kind, at(y_hi, 4)).start()

    def low_slots(hops):
        if hops in (0, 4):
            return [at(0, hops)]
        return [at(0, -hops), at(0, hops)]

    def from_cross(hops):
        for p in (0, 1):
            for k, slot in enumerate(low_slots(hops)):
                q = p if k == 0 else 1 - p
                arrived(kind_on, slot, q)
                to_pair(slot, q).start()
        for slot in low_slots(hops):
            to_sibling(kind_on, slot).start()

    def from_pair(hops):
        for slot in low_slots(hops):
            arrived(kind_swap, slot, 0)
            arrived(kind_swap, slot, 1)
            to_sibling(kind_swap, slot).start()


    def slot_at(steps, same):
        return ((x + steps + 4) % 4) * 2 + (y_lo if same else 1 - y_lo)

    def quarter(slot, q):
        return att.at[slot, pl.ds(q * QUARTER, QUARTER)]

    def send(slot, q, to_tp):
        return pltpu.make_async_remote_copy(
            src_ref=quarter(slot, q), dst_ref=quarter(slot, q), send_sem=sent.at[0],
            recv_sem=x_recv.at[slot, q], device_id=(ctx, to_tp), device_id_type=MESH,
        )

    x_to_right = lambda slot, q: send(slot, q, x_right)
    x_to_left = lambda slot, q: send(slot, q, x_left)
    x_to_pair = lambda slot, q: send(slot, q, pair)

    def landed_at(slot, q):
        x_to_pair(slot, q).wait_recv()

    def edge_copy(k):
        to_ctx = above if k == 0 else below
        src = teacher_ref.at[pl.ds(TEACH - EDGE, EDGE)] if k == 0 else teacher_ref.at[pl.ds(0, EDGE)]
        dst = ext.at[pl.ds(0, EDGE)] if k == 0 else ext.at[pl.ds(EDGE + TEACH, EDGE)]
        return pltpu.make_async_remote_copy(
            src_ref=src, dst_ref=dst, send_sem=sent.at[0], recv_sem=edge_recv.at[k],
            device_id=(to_ctx, tp), device_id_type=MESH,
        )

    def grad_copy(k):
        return pltpu.make_async_remote_copy(
            src_ref=edges.at[k], dst_ref=landed.at[k], send_sem=sent.at[0],
            recv_sem=edge_recv.at[2 + k], device_id=(above if k == 0 else below, tp),
            device_id_type=MESH,
        )

    def weight_load(slot):
        rows = pl.ds(pl.multiple_of(slot * DEPTH, DEPTH), DEPTH)
        return pltpu.make_async_copy(weight_ref.at[rows], weight.at[rows], load.at[5])

    student_load = pltpu.make_async_copy(student_ref, student, load.at[1])
    teacher_load = pltpu.make_async_copy(teacher_ref, ext.at[pl.ds(EDGE, TEACH)], load.at[2])
    def edge_and_loads():
        for k in range(2):
            edge_copy(k).start()
        student_load.start()
        teacher_load.start()
        for slot in range(8):
            weight_load(slot).start()

    half_rows = 2 * S_DEV

    def score(block, c, masked=False):
        cols = slice(c * half_rows, (c + 1) * half_rows)
        keys = buf[0, pl.ds(pl.multiple_of(block * 2 * S_DEV, 2 * S_DEV), 2 * S_DEV), :]
        s = jnp.dot(keys, q_t[:, cols], preferred_element_type=jnp.float32)
        if masked:
            key_pos = lax.broadcasted_iota(jnp.int32, s.shape, 0)
            query_pos = lax.broadcasted_iota(jnp.int32, s.shape, 1) % S_DEV + core * S_DEV
            s = jnp.where(key_pos <= query_pos, s, LOW)
        scores[c] = s
        new_peak = jnp.max(s, axis=0, keepdims=True)
        if not masked:
            old = peak[:, cols]
            new_peak = jnp.maximum(old, new_peak)
            decay[:, cols] = jnp.exp2((old - new_peak) * EXP_SCALE)
        peak[:, cols] = new_peak

    def gather_values(block, c, first=False):
        cols = slice(c * half_rows, (c + 1) * half_rows)
        weights = jnp.exp2((scores[c] - peak[:, cols]) * EXP_SCALE)
        added = jnp.sum(weights, axis=0, keepdims=True)
        rounded = weights.astype(jnp.bfloat16)
        base = block * 2 * S_DEV
        product = None
        for k in range(2):
            parts = [
                buf[1, pl.ds(pl.multiple_of(base + k * S_DEV + g * HD, HD), HD), :]
                for g in range(2)
            ]
            values = jnp.concatenate(parts, axis=1)
            term = jnp.dot(
                values, rounded[k * S_DEV : (k + 1) * S_DEV], preferred_element_type=jnp.float32
            )
            product = term if product is None else product + term
        if first:
            total[:, cols] = added
            accum[:, cols] = product
        else:
            shrink = decay[:, cols]
            total[:, cols] = total[:, cols] * shrink + added
            accum[:, cols] = accum[:, cols] * shrink + product

    own_block = ctx // 2
    from_sibling(ctx // 2)
    score(own_block, 0, masked=True)
    score(own_block, 1, masked=True)
    gather_values(own_block, 0, first=True)
    total[:, half_rows:] = jnp.zeros((1, half_rows), jnp.float32)
    accum[:, half_rows:] = jnp.zeros((HD, half_rows), jnp.float32)
    decay[:, half_rows:] = jnp.ones((1, half_rows), jnp.float32)

    low_order = {2: (1, -1), 3: (1, 1), 4: (1, -2), 5: (1, 2), 7: (1, -3), 8: (1, 3), 9: (1, 4)}
    low_events = {
        1: [(low_ring, 2), (low_ring, 1), (low_ring, 3), (low_ring, 4)], 2: [(from_pair, 1)],
        4: [(from_pair, 2)], 7: [(from_pair, 3)], 8: [(from_pair, 4)],
    }
    high_order = {
        1: (1, -1), 2: (1, 1), 3: (2, 0), 4: (1, -2), 5: (1, 2), 6: (2, -1), 7: (2, 1), 8: (1, -3),
        9: (1, 3), 10: (2, -2), 11: (2, 2), 12: (1, 4), 13: (2, -3), 14: (2, 3), 15: (2, 4),
    }
    high_events = {
        1: [(ring, 1), (from_cross, 0)], 2: [(ring, 2), (from_pair, 0)],
        3: [(from_cross, 1), (from_cross, 2)], 4: [(ring, 3)], 5: [(from_pair, 1), (from_pair, 2)],
        6: [(from_cross, 3), (from_cross, 4)], 7: [(ring, 4)], 9: [(from_pair, 3), (from_pair, 4)],
    }

    def lookup(n, field):
        low = pick(n, [low_order.get(k, (0, 0))[field] for k in range(16)])
        high = pick(n, [high_order.get(k, (0, 0))[field] for k in range(16)])
        return jnp.where(y_hi == 0, low, high)

    def step(n, before):
        plane = lookup(n, 0)
        block_z = (z + lookup(n, 1) + N_Z) % N_Z
        for hi, events in ((0, low_events), (1, high_events)):
            @pl.when(y_hi == hi)
            def _(events=events):
                for k, todo in events.items():
                    @pl.when(n == k)
                    def _(todo=todo):
                        for action, hops in todo:
                            action(hops)

        @pl.when(n == 9)
        def _():
            edge_and_loads()

        block = jnp.where(plane == 2, block_z, y_hi * N_Z + block_z)
        here = plane > 0

        @pl.when(here)
        def _():
            from_sibling(block)

        def compute(prior):
            score(block, 0)
            gather_values(prior, 1)
            score(block, 1)
            gather_values(block, 0)
            return block

        return lax.cond(here & (block < own_block), compute, lambda prior: prior, before)

    last_block = lax.fori_loop(1, 16, step, own_block)
    gather_values(last_block, 1)
    for h in range(4):
        cols = slice(h * S_DEV, (h + 1) * S_DEV)
        att[tp, :, h * HD : (h + 1) * HD] = (accum[:, cols] / total[:, cols]).T.astype(jnp.bfloat16)


    for q in range(2):
        x_to_right(tp, q).start()
        x_to_left(tp, q).start()
        x_to_pair(tp, 2 + q).start()
        send(tp, q, x_far).start()
    ext[WINDOW:, :] = jnp.zeros((ext.shape[0] - WINDOW, WIDTH), jnp.bfloat16)
    first = ctx * TEACH - EDGE
    start_load.wait()
    len_load.wait()
    start_row, len_row = starts[...], lens[...]
    row_pos = first + lax.broadcasted_iota(jnp.int32, (WINDOW, S_DEV), 0)
    inside = (row_pos >= start_row) & (row_pos < start_row + len_row)
    member_t[...] = jnp.where(inside, 1.0, 0.0).astype(jnp.bfloat16)
    wide_start = jnp.broadcast_to(start_row.astype(jnp.float32), (HD, S_DEV)).T[:, :1]
    wide_len = jnp.broadcast_to(len_row.astype(jnp.float32), (HD, S_DEV)).T
    counts[...] = 1.0 / wide_len
    col_pos = (first + lax.broadcasted_iota(jnp.int32, member.shape, 1)).astype(jnp.float32)
    inside = (col_pos >= wide_start) & (col_pos < wide_start + wide_len[:, :1])
    member[...] = jnp.where(inside, 1.0, 0.0).astype(jnp.bfloat16)
    student_load.wait()
    result[...] = student[...].astype(jnp.float32)

    def columns(j):
        return pl.ds(j * TILE, TILE)

    def multiply(slot):
        rows = pl.ds(pl.multiple_of(slot * DEPTH, DEPTH), DEPTH)

        result[...] += jnp.dot(att[slot], weight[rows, :], preferred_element_type=jnp.float32)

    prev, nxt = slot_at(-1, True), slot_at(1, True)
    far, far_other = slot_at(2, True), slot_at(2, False)
    prev_other, nxt_other = slot_at(-1, False), slot_at(1, False)

    for q in range(2):
        x_to_right(tp, 2 + q).start()
        x_to_left(tp, 2 + q).start()
        x_to_pair(tp, q).start()
    for q in (2, 3):
        landed_at(pair, q)
        x_to_right(pair, q).start()
        x_to_left(pair, q).start()
    pltpu.make_async_copy(weight_ref, weight, load.at[5]).wait()
    multiply(tp)
    for q in range(2):
        for slot in (prev, nxt):
            landed_at(slot, q)
            x_to_pair(slot, q).start()
    landed_at(prev, 2)
    x_to_right(prev, 2).start()
    landed_at(nxt, 3)
    x_to_left(nxt, 3).start()
    for q in range(2):
        landed_at(far, q)
        x_to_pair(far, q).start()
    teacher_load.wait()
    for k in range(2):
        edge_copy(k).wait_recv()

    summed = jnp.dot(member[...], ext[...], preferred_element_type=jnp.float32)
    target[...] = summed * counts[:, :1]

    landed_at(pair, 0)
    landed_at(pair, 1)
    landed_at(prev_other, 2)
    x_to_right(prev_other, 2).start()
    landed_at(nxt_other, 3)
    x_to_left(nxt_other, 3).start()
    multiply(pair)
    landed_at(prev, 3)
    multiply(prev)
    landed_at(nxt, 2)
    multiply(nxt)
    for q in (2, 3):
        landed_at(far, q)
    multiply(far)
    for q in (3, 0, 1):
        landed_at(prev_other, q)
    multiply(prev_other)
    for q in (2, 0, 1):
        landed_at(nxt_other, q)
    multiply(nxt_other)
    for q in (2, 3, 0, 1):
        landed_at(far_other, q)
    last_rows = pl.ds(pl.multiple_of(far_other * DEPTH, DEPTH), DEPTH)

    for j in range(WIDTH // TILE):
        student32 = result[:, columns(j)] + jnp.dot(
            att[far_other], weight[last_rows, columns(j)], preferred_element_type=jnp.float32
        )
        student[:, columns(j)] = student32.astype(jnp.bfloat16)
        weighted = ((student32 - target[:, columns(j)]) * counts[:, :1]).astype(jnp.bfloat16)
        spread = jnp.dot(member_t[...], weighted, preferred_element_type=jnp.float32)
        edges[0, :, columns(j)] = spread[EDGE + TEACH : EDGE + TEACH + HALO]
        edges[1, :, columns(j)] = spread[EDGE - HALO : EDGE]
        result[:, columns(j)] = spread[EDGE : EDGE + S_DEV]
        target[: TEACH - S_DEV, columns(j)] = spread[EDGE + S_DEV : EDGE + TEACH]

    for k in range(2):
        grad_copy(k).start()
    out_store = pltpu.make_async_copy(student, out_ref, load.at[0])
    out_store.start()
    ext[EDGE:S_DEV, :] = result[EDGE:, :].astype(jnp.bfloat16)
    rest = TEACH - S_DEV - EDGE
    ext[S_DEV : TEACH - EDGE, :] = target[:rest, :].astype(jnp.bfloat16)
    grad_stores = [
        pltpu.make_async_copy(ext.at[part], grad_ref.at[part], load.at[1 + k])
        for k, part in enumerate(
            (pl.ds(EDGE, TEACH - 2 * EDGE), pl.ds(0, EDGE), pl.ds(TEACH - EDGE, EDGE))
        )
    ]
    grad_stores[0].start()
    for k in range(2):
        grad_copy(k).wait_recv()
    low = result[:EDGE, :] + jnp.concatenate([landed[0], jnp.zeros_like(landed[0])], axis=0)
    ext[:EDGE, :] = low.astype(jnp.bfloat16)
    grad_stores[1].start()
    high = target[rest : rest + EDGE, :] + jnp.concatenate(
        [jnp.zeros_like(landed[1]), landed[1]], axis=0
    )
    ext[TEACH - EDGE : TEACH, :] = high.astype(jnp.bfloat16)
    grad_stores[2].start()

    out_store.wait()
    for store in grad_stores:
        store.wait()

    def all_sent(pieces):
        rows = weight.at[pl.ds(0, pieces * 16)]
        pltpu.make_async_remote_copy(
            src_ref=rows, dst_ref=rows, send_sem=sent.at[0], recv_sem=edge_recv.at[0],
            device_id=(sibling, tp), device_id_type=MESH,
        ).wait_send()

    @pl.when(y_hi == 0)
    def _():
        all_sent(14 + 16 + 14 + 32 + 60)

    @pl.when(y_hi == 1)
    def _():
        all_sent(28 + 16 + 64 + 60)


def place_kernel(rows_in, grad_in, out_ref, grad_ref, rows, grad, sems):
    pairs = []
    for source, middle, result in ((rows_in, rows, out_ref), (grad_in, grad, grad_ref)):
        for k in range(2):
            size = source.shape[0] // 2
            part = pl.ds(k * size, size)
            at = len(pairs)
            pairs.append((
                pltpu.make_async_copy(source.at[part], middle.at[part], sems.at[0, at]),
                pltpu.make_async_copy(middle.at[part], result.at[part], sems.at[1, at]),
            ))
    for fetch, _ in pairs:
        fetch.start()
    for fetch, store in pairs:
        fetch.wait()
        store.start()
    for _, store in pairs:
        store.wait()


def body(student_rows, queries, keys_values, out_weight, teacher_rows, span_start, span_len):
    anywhere = pl.BlockSpec(memory_space=pl.ANY)
    dma = pltpu.SemaphoreType.DMA
    bf16, f32 = jnp.bfloat16, jnp.float32
    wide = 4 * S_DEV
    results = (
        jax.ShapeDtypeStruct((S_DEV, WIDTH), bf16),
        jax.ShapeDtypeStruct((TEACH, WIDTH), bf16),
    )
    rows, grad = pl.pallas_call(
        layer_kernel,
        out_shape=results,
        in_specs=[anywhere] * 7,
        out_specs=(anywhere, anywhere),
        scratch_shapes=[
            pltpu.VMEM((2, 32 * S_DEV, HD), bf16),
            pltpu.VMEM((S_DEV, HD), bf16),
            pltpu.VMEM((S_DEV, DEPTH), bf16),
            pltpu.VMEM((HD, wide), bf16),
            pltpu.VMEM((2, 2 * S_DEV, wide // 2), f32),
            pltpu.VMEM((1, wide), f32),
            pltpu.VMEM((1, wide), f32),
            pltpu.VMEM((1, wide), f32),
            pltpu.VMEM((HD, wide), f32),
            pltpu.VMEM((8, S_DEV, DEPTH), bf16),
            pltpu.VMEM((8 * DEPTH, WIDTH), bf16),
            pltpu.VMEM((S_DEV, WIDTH), bf16),
            pltpu.VMEM((512, WIDTH), bf16),
            pltpu.VMEM((S_DEV, 512), bf16),
            pltpu.VMEM((WINDOW, S_DEV), bf16),
            pltpu.VMEM((S_DEV, WIDTH), f32),
            pltpu.VMEM((S_DEV, WIDTH), f32),
            pltpu.VMEM((S_DEV, HD), f32),
            pltpu.VMEM((2, HALO, WIDTH), f32),
            pltpu.VMEM((2, HALO, WIDTH), f32),
            pltpu.VMEM((1, S_DEV), jnp.int32),
            pltpu.VMEM((1, S_DEV), jnp.int32),
            dma((2, 32)), dma((16,)), dma((1,)), dma((8, 4)), dma((8,)), dma((4,)),
        ],
        compiler_params=pltpu.CompilerParams(
            collective_id=0, has_side_effects=True, vmem_limit_bytes=60 << 20
        ),
        name="layer",
    )(
        queries, keys_values, student_rows, out_weight, teacher_rows,
        span_start.reshape(1, S_DEV), span_len.reshape(1, S_DEV),
    )
    return pl.pallas_call(
        place_kernel,
        out_shape=results,
        in_specs=[anywhere] * 2,
        out_specs=(anywhere, anywhere),
        scratch_shapes=[
            pltpu.VMEM((S_DEV, WIDTH), bf16),
            pltpu.VMEM((TEACH, WIDTH), bf16),
            dma((2, 4)),
        ],
        compiler_params=pltpu.CompilerParams(vmem_limit_bytes=60 << 20),
        name="place",
    )(rows, grad)


def solution(mesh):
    return jax.shard_map(
        body,
        mesh=mesh,
        in_specs=(
            P("ctx", "tp"),
            P("ctx", "tp"),
            P(None, "ctx", None),
            P(None, "tp"),
            P("ctx", "tp"),
            P("ctx"),
            P("ctx"),
        ),
        out_specs=(P("ctx", "tp"), P("ctx", "tp")),
        check_vma=False,
    )
```

```python
import functools
import math

import jax
import jax.numpy as jnp
from jax import lax
from jax.experimental import pallas as pl
from jax.experimental.pallas import tpu as pltpu
from jax.sharding import PartitionSpec as P

HD = 128
S_DEV = 256
HALO = 8
N_Z = 8
MESH = pl.DeviceIdType.MESH
EXP_SCALE = math.log2(math.e) / math.sqrt(HD)
LOW = -1e30

TEACH = 384
EDGE = 16
WINDOW = TEACH + 2 * EDGE
DEPTH = 512
WIDTH = 1024
QUARTER = S_DEV // 4
TILE = 256


def pick(step, table):
    value = table[0]
    for k in range(1, len(table)):
        value = jnp.where(step == k, table[k], value)
    return value


def layer_kernel(
    q_ref, kv_ref, student_ref, weight_ref, teacher_ref, start_ref, len_ref, out_ref, grad_ref,
    buf, own_v, q_rows, q_t, scores, peak, decay, total, accum,
    att, weight, student, ext, member, member_t, result, target, counts, edges, landed,
    starts, lens, recv, recv_sib, sent, x_recv, load, edge_recv,
):
    ctx, tp = lax.axis_index("ctx"), lax.axis_index("tp")
    core, z, y_hi = ctx % 2, (ctx // 2) % N_Z, ctx // 16
    x, y_lo = tp // 2, tp % 2
    sibling = ctx + 1 - 2 * core
    right = y_hi * 16 + ((z + 1) % N_Z) * 2 + core
    left = y_hi * 16 + ((z + N_Z - 1) % N_Z) * 2 + core
    other_hi = (ctx + 16) % 32
    pair = tp + 1 - 2 * y_lo
    kind_on = jnp.where(y_hi == 0, y_lo, 1 - y_lo)
    kind_swap = 1 - kind_on
    x_right, x_left = ((x + 1) % 4) * 2 + y_lo, ((x + 3) % 4) * 2 + y_lo
    x_far = ((x + 2) % 4) * 2 + y_lo
    above, below = (ctx + 1) % 32, (ctx + 31) % 32
    has_above, has_below = ctx < 31, ctx > 0

    def at(hi, steps):
        return hi * 16 + ((z + steps + N_Z) % N_Z) * 2 + core

    def piece(kind, slot, p):
        return buf.at[kind, pl.ds(pl.multiple_of(slot * S_DEV + p * HD, HD), HD)]

    def part(kind, slot):
        return buf.at[kind, pl.ds(pl.multiple_of(slot * S_DEV, S_DEV), S_DEV)]

    def copy(kind, slot, p, to_ctx, to_tp):
        return pltpu.make_async_remote_copy(
            src_ref=piece(kind, slot, p), dst_ref=piece(kind, slot, p), send_sem=sent.at[0],
            recv_sem=recv.at[kind, slot // 2 * 2 + p], device_id=(to_ctx, to_tp), device_id_type=MESH,
        )

    def arrived(kind, slot, p):
        copy(kind, slot, p, ctx, pair).wait_recv()

    def to_sibling(kind, slot):
        return pltpu.make_async_remote_copy(
            src_ref=part(kind, slot), dst_ref=part(kind, slot), send_sem=sent.at[0],
            recv_sem=recv_sib.at[slot // 2], device_id=(sibling, tp), device_id_type=MESH,
        )

    def from_sibling(block):
        both = buf.at[0, pl.ds(0, 2 * S_DEV)]
        pltpu.make_async_remote_copy(
            src_ref=both, dst_ref=both, send_sem=sent.at[0], recv_sem=recv_sib.at[block],
            device_id=(sibling, tp), device_id_type=MESH,
        ).wait_recv()

    def to_right(kind, hops, p):
        return copy(kind, at(y_hi, -hops), p, right, tp)

    def to_left(kind, hops, p):
        return copy(kind, at(y_hi, hops), p, left, tp)

    def to_second(slot, p, steps):
        return copy(y_lo, slot, p, at(y_hi, steps), tp)

    def to_cross(slot, p):
        return copy(y_lo, slot, p, other_hi, pair)

    def to_pair(slot, p):
        return copy(kind_on, slot, p, ctx, pair)

    k_load = pltpu.make_async_copy(
        kv_ref.at[0, :, pl.ds(pl.multiple_of(x * HD, HD), HD)], part(0, ctx), load.at[3]
    )
    v_load = pltpu.make_async_copy(
        kv_ref.at[1, :, pl.ds(pl.multiple_of(x * HD, HD), HD)], own_v, load.at[0]
    )
    q_load = pltpu.make_async_copy(q_ref, q_rows, load.at[4])
    start_load = pltpu.make_async_copy(start_ref, starts, load.at[6])
    len_load = pltpu.make_async_copy(len_ref, lens, load.at[7])
    v_load.start()
    k_load.start()
    q_load.start()
    start_load.start()
    len_load.start()
    barrier = pltpu.get_barrier_semaphore()
    for to_ctx, to_tp in (
        (right, tp), (left, tp), (sibling, tp), (other_hi, pair), (ctx, pair),
        (ctx, x_right), (ctx, x_left), (ctx, x_far),
        (at(y_hi, 2), tp), (at(y_hi, -2), tp),
    ):
        pl.semaphore_signal(barrier, inc=1, device_id=(to_ctx, to_tp), device_id_type=MESH)
    for there, to_ctx in ((has_above, above), (has_below, below)):
        @pl.when(there)
        def _(to_ctx=to_ctx):
            pl.semaphore_signal(barrier, inc=1, device_id=(to_ctx, tp), device_id_type=MESH)

    v_load.wait()
    v_own = own_v[...].astype(jnp.float32)
    for half in range(2):
        turned = v_own[half * HD : (half + 1) * HD].T.astype(jnp.bfloat16)
        start = pl.multiple_of(ctx * S_DEV + half * HD, HD)
        buf[1, pl.ds(start, HD), :] = turned
    k_load.wait()
    pl.semaphore_wait(barrier, jnp.where(has_above & has_below, 12, 11))

    def start_near(kind):
        for p in range(2):
            to_right(kind, 0, p).start()
            to_left(kind, 0, 1 - p).start()

    @pl.when(y_hi == 0)
    def _():
        for p in range(2):
            to_second(ctx, p, 2).start()
            to_second(ctx, 1 - p, -2).start()
            to_cross(ctx, p).start()

    @pl.when(y_hi == 1)
    def _():
        start_near(0)

    for kind in range(2):
        to_sibling(kind, ctx).start()

    q_load.wait()
    for h in range(4):
        q_t[:, h * S_DEV : (h + 1) * S_DEV] = (
            q_rows[:, h * HD : (h + 1) * HD].astype(jnp.float32).T.astype(jnp.bfloat16)
        )

    @pl.when(y_hi == 0)
    def _():
        start_near(y_lo)

    @pl.when(y_hi == 1)
    def _():
        start_near(1)

    def low_ring(hops):
        def side(sign, p):
            slot = at(0, sign * hops)
            arrived(y_lo, slot, p)
            if hops == 2:
                copy(y_lo, slot, p, left if sign > 0 else right, tp).start()
                if (p == 0) == (sign < 0):
                    to_second(slot, p, -2 * sign).start()
            to_cross(slot, p).start()
            to_pair(slot, p).start()

        for p in range(2):
            side(-1, p)
            if hops < 4:
                side(1, 1 - p)
        for slot in low_slots(hops):
            to_sibling(y_lo, slot).start()

    def ring(hops):
        def side(kind, moving_right, p):
            arrived(kind, at(y_hi, -hops if moving_right else hops), p)
            last = 3 if (p == 0) == moving_right else 2
            if hops <= last:
                (to_right if moving_right else to_left)(kind, hops, p).start()

        kinds = range(2)
        if hops < 4:
            for kind in kinds:
                for k in range(2):
                    side(kind, True, k)
                    side(kind, False, 1 - k)
            for kind in kinds:
                to_sibling(kind, at(y_hi, -hops)).start()
                to_sibling(kind, at(y_hi, hops)).start()
        else:
            for kind in kinds:
                side(kind, True, 0)
                side(kind, False, 1)
                to_sibling(kind, at(y_hi, 4)).start()

    def low_slots(hops):
        if hops in (0, 4):
            return [at(0, hops)]
        return [at(0, -hops), at(0, hops)]

    def from_cross(hops):
        for p in (0, 1):
            for k, slot in enumerate(low_slots(hops)):
                q = p if k == 0 else 1 - p
                arrived(kind_on, slot, q)
                to_pair(slot, q).start()
        for slot in low_slots(hops):
            to_sibling(kind_on, slot).start()

    def from_pair(hops):
        for slot in low_slots(hops):
            arrived(kind_swap, slot, 0)
            arrived(kind_swap, slot, 1)
            to_sibling(kind_swap, slot).start()


    def slot_at(steps, same):
        return ((x + steps + 4) % 4) * 2 + (y_lo if same else 1 - y_lo)

    def quarter(slot, q):
        return att.at[slot, pl.ds(q * QUARTER, QUARTER)]

    def send(slot, q, to_tp):
        return pltpu.make_async_remote_copy(
            src_ref=quarter(slot, q), dst_ref=quarter(slot, q), send_sem=sent.at[0],
            recv_sem=x_recv.at[slot, q], device_id=(ctx, to_tp), device_id_type=MESH,
        )

    x_to_right = lambda slot, q: send(slot, q, x_right)
    x_to_left = lambda slot, q: send(slot, q, x_left)
    x_to_pair = lambda slot, q: send(slot, q, pair)

    def landed_at(slot, q):
        x_to_pair(slot, q).wait_recv()

    def edge_copy(k):
        to_ctx = above if k == 0 else below
        src = teacher_ref.at[pl.ds(TEACH - EDGE, EDGE)] if k == 0 else teacher_ref.at[pl.ds(0, EDGE)]
        dst = ext.at[pl.ds(0, EDGE)] if k == 0 else ext.at[pl.ds(EDGE + TEACH, EDGE)]
        return pltpu.make_async_remote_copy(
            src_ref=src, dst_ref=dst, send_sem=sent.at[0], recv_sem=edge_recv.at[k],
            device_id=(to_ctx, tp), device_id_type=MESH,
        )

    def grad_copy(k, half):
        part = pl.ds(half * (WIDTH // 2), WIDTH // 2)
        return pltpu.make_async_remote_copy(
            src_ref=edges.at[k, :, part], dst_ref=landed.at[k, :, part], send_sem=sent.at[0],
            recv_sem=edge_recv.at[2 + 2 * k + half], device_id=(above if k == 0 else below, tp),
            device_id_type=MESH,
        )

    def weight_load(slot):
        rows = pl.ds(pl.multiple_of(slot * DEPTH, DEPTH), DEPTH)
        return pltpu.make_async_copy(weight_ref.at[rows], weight.at[rows], load.at[5])

    student_load = pltpu.make_async_copy(student_ref, student, load.at[1])
    teacher_load = pltpu.make_async_copy(teacher_ref, ext.at[pl.ds(EDGE, TEACH)], load.at[2])
    def edge_and_loads():
        for k, there in ((0, has_above), (1, has_below)):
            @pl.when(there)
            def _(k=k):
                edge_copy(k).start()

        student_load.start()
        teacher_load.start()
        for slot in range(8):
            weight_load(slot).start()

    half_rows = 2 * S_DEV

    def score(block, c, masked=False):
        cols = slice(c * half_rows, (c + 1) * half_rows)
        keys = buf[0, pl.ds(pl.multiple_of(block * 2 * S_DEV, 2 * S_DEV), 2 * S_DEV), :]
        s = jnp.dot(keys, q_t[:, cols], preferred_element_type=jnp.float32)
        if masked:
            key_pos = lax.broadcasted_iota(jnp.int32, s.shape, 0)
            query_pos = lax.broadcasted_iota(jnp.int32, s.shape, 1) % S_DEV + core * S_DEV
            s = jnp.where(key_pos <= query_pos, s, LOW)
        scores[c] = s
        new_peak = jnp.max(s, axis=0, keepdims=True)
        if not masked:
            old = peak[:, cols]
            new_peak = jnp.maximum(old, new_peak)
            decay[:, cols] = jnp.exp2((old - new_peak) * EXP_SCALE)
        peak[:, cols] = new_peak

    def gather_values(block, c, first=False):
        cols = slice(c * half_rows, (c + 1) * half_rows)
        weights = jnp.exp2((scores[c] - peak[:, cols]) * EXP_SCALE)
        added = jnp.sum(weights, axis=0, keepdims=True)
        rounded = weights.astype(jnp.bfloat16)
        base = block * 2 * S_DEV
        product = None
        for k in range(2):
            parts = [
                buf[1, pl.ds(pl.multiple_of(base + k * S_DEV + g * HD, HD), HD), :]
                for g in range(2)
            ]
            values = jnp.concatenate(parts, axis=1)
            term = jnp.dot(
                values, rounded[k * S_DEV : (k + 1) * S_DEV], preferred_element_type=jnp.float32
            )
            product = term if product is None else product + term
        if first:
            total[:, cols] = added
            accum[:, cols] = product
        else:
            shrink = decay[:, cols]
            total[:, cols] = total[:, cols] * shrink + added
            accum[:, cols] = accum[:, cols] * shrink + product

    own_block = ctx // 2
    from_sibling(ctx // 2)
    score(own_block, 0, masked=True)
    score(own_block, 1, masked=True)
    gather_values(own_block, 0, first=True)
    total[:, half_rows:] = jnp.zeros((1, half_rows), jnp.float32)
    accum[:, half_rows:] = jnp.zeros((HD, half_rows), jnp.float32)
    decay[:, half_rows:] = jnp.ones((1, half_rows), jnp.float32)

    low_order = {2: (1, -1), 3: (1, 1), 4: (1, -2), 5: (1, 2), 7: (1, -3), 8: (1, 3), 9: (1, 4)}
    low_events = {
        1: [(low_ring, 2), (low_ring, 1), (low_ring, 3), (low_ring, 4)], 2: [(from_pair, 1)],
        4: [(from_pair, 2)], 7: [(from_pair, 3)], 8: [(from_pair, 4)],
    }
    high_order = {
        1: (1, -1), 2: (1, 1), 3: (2, 0), 4: (1, -2), 5: (1, 2), 6: (1, -3), 7: (1, 3), 8: (2, -1),
        9: (2, 1), 10: (2, -2), 11: (2, 2), 12: (1, 4), 13: (2, -3), 14: (2, 3), 15: (2, 4),
    }
    high_events = {
        1: [(ring, 1), (from_cross, 0)], 3: [(ring, 2), (from_pair, 0)],
        4: [(from_cross, 1), (from_cross, 2)], 6: [(ring, 3)], 7: [(from_cross, 3)],
        8: [(from_cross, 4), (from_pair, 1), (from_pair, 2)], 11: [(ring, 4)],
        12: [(from_pair, 3)], 13: [(from_pair, 4)],
    }

    def lookup(n, field):
        low = pick(n, [low_order.get(k, (0, 0))[field] for k in range(16)])
        high = pick(n, [high_order.get(k, (0, 0))[field] for k in range(16)])
        return jnp.where(y_hi == 0, low, high)

    def step(n, before):
        plane = lookup(n, 0)
        block_z = (z + lookup(n, 1) + N_Z) % N_Z
        for hi, events in ((0, low_events), (1, high_events)):
            @pl.when(y_hi == hi)
            def _(events=events):
                for k, todo in events.items():
                    @pl.when(n == k)
                    def _(todo=todo):
                        for action, hops in todo:
                            action(hops)

        @pl.when(n == 9)
        def _():
            edge_and_loads()

        block = jnp.where(plane == 2, block_z, y_hi * N_Z + block_z)
        here = plane > 0

        @pl.when(here)
        def _():
            from_sibling(block)

        def compute(prior):
            score(block, 0)
            gather_values(prior, 1)
            score(block, 1)
            gather_values(block, 0)
            return block

        return lax.cond(here & (block < own_block), compute, lambda prior: prior, before)

    last_block = lax.fori_loop(1, 16, step, own_block)
    gather_values(last_block, 1)
    for h in range(4):
        cols = slice(h * S_DEV, (h + 1) * S_DEV)
        att[tp, :, h * HD : (h + 1) * HD] = (accum[:, cols] / total[:, cols]).T.astype(jnp.bfloat16)


    for q in range(2):
        x_to_right(tp, q).start()
        x_to_left(tp, q).start()
        x_to_pair(tp, 2 + q).start()
    @pl.when(ctx == 0)
    def _():
        ext[:EDGE, :] = jnp.zeros((EDGE, WIDTH), jnp.bfloat16)
        landed[0] = jnp.zeros((HALO, WIDTH), jnp.float32)

    @pl.when(ctx == 31)
    def _():
        ext[EDGE + TEACH : WINDOW, :] = jnp.zeros((EDGE, WIDTH), jnp.bfloat16)
        landed[1] = jnp.zeros((HALO, WIDTH), jnp.float32)

    ext[WINDOW:, :] = jnp.zeros((ext.shape[0] - WINDOW, WIDTH), jnp.bfloat16)
    first = ctx * TEACH - EDGE
    start_load.wait()
    len_load.wait()
    start_row, len_row = starts[...], lens[...]
    row_pos = first + lax.broadcasted_iota(jnp.int32, (WINDOW, S_DEV), 0)
    inside = (row_pos >= start_row) & (row_pos < start_row + len_row)
    member_t[...] = jnp.where(inside, 1.0, 0.0).astype(jnp.bfloat16)
    for q in range(2):
        send(tp, q, x_far).start()
        x_to_pair(tp, q).start()
    wide_start = jnp.broadcast_to(start_row.astype(jnp.float32), (HD, S_DEV)).T[:, :1]
    wide_len = jnp.broadcast_to(len_row.astype(jnp.float32), (HD, S_DEV)).T
    counts[...] = 1.0 / wide_len
    col_pos = (first + lax.broadcasted_iota(jnp.int32, member.shape, 1)).astype(jnp.float32)
    inside = (col_pos >= wide_start) & (col_pos < wide_start + wide_len[:, :1])
    member[...] = jnp.where(inside, 1.0, 0.0).astype(jnp.bfloat16)
    student_load.wait()
    result[...] = student[...].astype(jnp.float32)

    def columns(j):
        return pl.ds(j * TILE, TILE)

    def multiply(slot):
        rows = pl.ds(pl.multiple_of(slot * DEPTH, DEPTH), DEPTH)

        result[...] += jnp.dot(att[slot], weight[rows, :], preferred_element_type=jnp.float32)

    prev, nxt = slot_at(-1, True), slot_at(1, True)
    far, far_other = slot_at(2, True), slot_at(2, False)
    prev_other, nxt_other = slot_at(-1, False), slot_at(1, False)

    for q in range(2):
        x_to_right(tp, 2 + q).start()
        x_to_left(tp, 2 + q).start()
    for q in (2, 3):
        landed_at(pair, q)
        x_to_right(pair, q).start()
        x_to_left(pair, q).start()
    pltpu.make_async_copy(weight_ref, weight, load.at[5]).wait()
    multiply(tp)
    for q in range(2):
        for slot in (prev, nxt):
            landed_at(slot, q)
            x_to_pair(slot, q).start()
    landed_at(prev, 2)
    x_to_right(prev, 2).start()
    landed_at(nxt, 3)
    x_to_left(nxt, 3).start()
    for q in range(2):
        landed_at(far, q)
        x_to_pair(far, q).start()
    teacher_load.wait()
    for k, there in ((0, has_below), (1, has_above)):
        @pl.when(there)
        def _(k=k):
            edge_copy(k).wait_recv()


    summed = jnp.dot(member[...], ext[...], preferred_element_type=jnp.float32)
    target[...] = summed * counts[:, :1]

    landed_at(pair, 0)
    landed_at(pair, 1)
    landed_at(prev_other, 2)
    x_to_right(prev_other, 2).start()
    landed_at(nxt_other, 3)
    x_to_left(nxt_other, 3).start()
    multiply(pair)
    landed_at(prev, 3)
    multiply(prev)
    landed_at(nxt, 2)
    multiply(nxt)
    for q in (2, 3):
        landed_at(far, q)
    multiply(far)
    for q in (3, 0, 1):
        landed_at(prev_other, q)
    multiply(prev_other)
    for q in (2, 0, 1):
        landed_at(nxt_other, q)
    multiply(nxt_other)
    for q in (2, 3, 0, 1):
        landed_at(far_other, q)
    last_rows = pl.ds(pl.multiple_of(far_other * DEPTH, DEPTH), DEPTH)

    for j in range(WIDTH // TILE):
        student32 = result[:, columns(j)] + jnp.dot(
            att[far_other], weight[last_rows, columns(j)], preferred_element_type=jnp.float32
        )
        student[:, columns(j)] = student32.astype(jnp.bfloat16)
        weighted = ((student32 - target[:, columns(j)]) * counts[:, :1]).astype(jnp.bfloat16)
        spread = jnp.dot(member_t[...], weighted, preferred_element_type=jnp.float32)
        edges[0, :, columns(j)] = spread[EDGE + TEACH : EDGE + TEACH + HALO]
        edges[1, :, columns(j)] = spread[EDGE - HALO : EDGE]
        result[:, columns(j)] = spread[EDGE : EDGE + S_DEV]
        target[: TEACH - S_DEV, columns(j)] = spread[EDGE + S_DEV : EDGE + TEACH]
        if j % 2 == 1:
            for k, there in ((0, has_above), (1, has_below)):
                @pl.when(there)
                def _(k=k, j=j):
                    grad_copy(k, j // 2).start()


    out_store = pltpu.make_async_copy(student, out_ref, load.at[0])
    out_store.start()
    ext[EDGE:S_DEV, :] = result[EDGE:, :].astype(jnp.bfloat16)
    rest = TEACH - S_DEV - EDGE
    ext[S_DEV : TEACH - EDGE, :] = target[:rest, :].astype(jnp.bfloat16)
    grad_stores = [
        pltpu.make_async_copy(ext.at[part], grad_ref.at[part], load.at[1 + k])
        for k, part in enumerate(
            (pl.ds(EDGE, TEACH - 2 * EDGE), pl.ds(0, EDGE), pl.ds(TEACH - EDGE, EDGE))
        )
    ]
    grad_stores[0].start()
    for k, there in ((0, has_below), (1, has_above)):
        @pl.when(there)
        def _(k=k):
            for half in range(2):
                grad_copy(k, half).wait_recv()

    low = result[:EDGE, :] + jnp.concatenate([landed[0], jnp.zeros_like(landed[0])], axis=0)
    ext[:EDGE, :] = low.astype(jnp.bfloat16)
    grad_stores[1].start()
    high = target[rest : rest + EDGE, :] + jnp.concatenate(
        [jnp.zeros_like(landed[1]), landed[1]], axis=0
    )
    ext[TEACH - EDGE : TEACH, :] = high.astype(jnp.bfloat16)
    grad_stores[2].start()

    out_store.wait()
    for store in grad_stores:
        store.wait()

    def all_sent(pieces):
        rows = weight.at[pl.ds(0, pieces * 16)]
        pltpu.make_async_remote_copy(
            src_ref=rows, dst_ref=rows, send_sem=sent.at[0], recv_sem=edge_recv.at[0],
            device_id=(sibling, tp), device_id_type=MESH,
        ).wait_send()

    for hi, pieces in ((0, 14 + 16 + 14 + 32 + 56), (1, 28 + 16 + 64 + 56)):
        inner = has_above & has_below

        @pl.when((y_hi == hi) & inner)
        def _(pieces=pieces):
            all_sent(pieces + 4)

        @pl.when((y_hi == hi) & ~inner)
        def _(pieces=pieces):
            all_sent(pieces + 2)


def place_kernel(rows_in, grad_in, out_ref, grad_ref, rows, grad, sems):
    pairs = []
    for source, middle, result in ((rows_in, rows, out_ref), (grad_in, grad, grad_ref)):
        for k in range(2):
            size = source.shape[0] // 2
            part = pl.ds(k * size, size)
            at = len(pairs)
            pairs.append((
                pltpu.make_async_copy(source.at[part], middle.at[part], sems.at[0, at]),
                pltpu.make_async_copy(middle.at[part], result.at[part], sems.at[1, at]),
            ))
    for fetch, _ in pairs:
        fetch.start()
    for fetch, store in pairs:
        fetch.wait()
        store.start()
    for _, store in pairs:
        store.wait()


def body(student_rows, queries, keys_values, out_weight, teacher_rows, span_start, span_len):
    anywhere = pl.BlockSpec(memory_space=pl.ANY)
    dma = pltpu.SemaphoreType.DMA
    bf16, f32 = jnp.bfloat16, jnp.float32
    wide = 4 * S_DEV
    results = (
        jax.ShapeDtypeStruct((S_DEV, WIDTH), bf16),
        jax.ShapeDtypeStruct((TEACH, WIDTH), bf16),
    )
    rows, grad = pl.pallas_call(
        layer_kernel,
        out_shape=results,
        in_specs=[anywhere] * 7,
        out_specs=(anywhere, anywhere),
        scratch_shapes=[
            pltpu.VMEM((2, 32 * S_DEV, HD), bf16),
            pltpu.VMEM((S_DEV, HD), bf16),
            pltpu.VMEM((S_DEV, DEPTH), bf16),
            pltpu.VMEM((HD, wide), bf16),
            pltpu.VMEM((2, 2 * S_DEV, wide // 2), f32),
            pltpu.VMEM((1, wide), f32),
            pltpu.VMEM((1, wide), f32),
            pltpu.VMEM((1, wide), f32),
            pltpu.VMEM((HD, wide), f32),
            pltpu.VMEM((8, S_DEV, DEPTH), bf16),
            pltpu.VMEM((8 * DEPTH, WIDTH), bf16),
            pltpu.VMEM((S_DEV, WIDTH), bf16),
            pltpu.VMEM((512, WIDTH), bf16),
            pltpu.VMEM((S_DEV, 512), bf16),
            pltpu.VMEM((WINDOW, S_DEV), bf16),
            pltpu.VMEM((S_DEV, WIDTH), f32),
            pltpu.VMEM((S_DEV, WIDTH), f32),
            pltpu.VMEM((S_DEV, HD), f32),
            pltpu.VMEM((2, HALO, WIDTH), f32),
            pltpu.VMEM((2, HALO, WIDTH), f32),
            pltpu.VMEM((1, S_DEV), jnp.int32),
            pltpu.VMEM((1, S_DEV), jnp.int32),
            dma((2, 32)), dma((16,)), dma((1,)), dma((8, 4)), dma((8,)), dma((6,)),
        ],
        compiler_params=pltpu.CompilerParams(
            collective_id=0, has_side_effects=True, vmem_limit_bytes=60 << 20
        ),
        name="layer",
    )(
        queries, keys_values, student_rows, out_weight, teacher_rows,
        span_start.reshape(1, S_DEV), span_len.reshape(1, S_DEV),
    )
    return pl.pallas_call(
        place_kernel,
        out_shape=results,
        in_specs=[anywhere] * 2,
        out_specs=(anywhere, anywhere),
        scratch_shapes=[
            pltpu.VMEM((S_DEV, WIDTH), bf16),
            pltpu.VMEM((TEACH, WIDTH), bf16),
            dma((2, 4)),
        ],
        compiler_params=pltpu.CompilerParams(vmem_limit_bytes=60 << 20),
        name="place",
    )(rows, grad)


def solution(mesh):
    return jax.shard_map(
        body,
        mesh=mesh,
        in_specs=(
            P("ctx", "tp"),
            P("ctx", "tp"),
            P(None, "ctx", None),
            P(None, "tp"),
            P("ctx", "tp"),
            P("ctx"),
            P("ctx"),
        ),
        out_specs=(P("ctx", "tp"), P("ctx", "tp")),
        check_vma=False,
    )
```

```python
import functools
import math

import jax
import jax.numpy as jnp
from jax import lax
from jax.experimental import pallas as pl
from jax.experimental.pallas import tpu as pltpu
from jax.sharding import PartitionSpec as P

HD = 128
S_DEV = 256
HALO = 8
N_Z = 8
MESH = pl.DeviceIdType.MESH
EXP_SCALE = math.log2(math.e) / math.sqrt(HD)
LOW = -1e30

TEACH = 384
EDGE = 16
WINDOW = TEACH + 2 * EDGE
DEPTH = 512
WIDTH = 1024
QUARTER = S_DEV // 4
TILE = 256


def pick(step, table):
    value = table[0]
    for k in range(1, len(table)):
        value = jnp.where(step == k, table[k], value)
    return value


def layer_kernel(
    q_ref, kv_ref, student_ref, weight_ref, teacher_ref, start_ref, len_ref, out_ref, grad_ref,
    buf, own_v, q_rows, q_t, scores, peak, decay, total, accum,
    att, weight, student, ext, member, member_t, result, target, counts, edges, landed,
    starts, lens, recv, recv_sib, sent, x_recv, load, edge_recv,
):
    ctx, tp = lax.axis_index("ctx"), lax.axis_index("tp")
    core, z, y_hi = ctx % 2, (ctx // 2) % N_Z, ctx // 16
    x, y_lo = tp // 2, tp % 2
    sibling = ctx + 1 - 2 * core
    right = y_hi * 16 + ((z + 1) % N_Z) * 2 + core
    left = y_hi * 16 + ((z + N_Z - 1) % N_Z) * 2 + core
    other_hi = (ctx + 16) % 32
    pair = tp + 1 - 2 * y_lo
    kind_on = jnp.where(y_hi == 0, y_lo, 1 - y_lo)
    kind_swap = 1 - kind_on
    x_right, x_left = ((x + 1) % 4) * 2 + y_lo, ((x + 3) % 4) * 2 + y_lo
    x_far = ((x + 2) % 4) * 2 + y_lo
    above, below = (ctx + 1) % 32, (ctx + 31) % 32
    has_above, has_below = ctx < 31, ctx > 0

    def at(hi, steps):
        return hi * 16 + ((z + steps + N_Z) % N_Z) * 2 + core

    def piece(kind, slot, p):
        return buf.at[kind, pl.ds(pl.multiple_of(slot * S_DEV + p * HD, HD), HD)]

    def part(kind, slot):
        return buf.at[kind, pl.ds(pl.multiple_of(slot * S_DEV, S_DEV), S_DEV)]

    def copy(kind, slot, p, to_ctx, to_tp):
        return pltpu.make_async_remote_copy(
            src_ref=piece(kind, slot, p), dst_ref=piece(kind, slot, p), send_sem=sent.at[0],
            recv_sem=recv.at[kind, slot // 2 * 2 + p], device_id=(to_ctx, to_tp), device_id_type=MESH,
        )

    def arrived(kind, slot, p):
        copy(kind, slot, p, ctx, pair).wait_recv()

    def to_sibling(kind, slot):
        return pltpu.make_async_remote_copy(
            src_ref=part(kind, slot), dst_ref=part(kind, slot), send_sem=sent.at[0],
            recv_sem=recv_sib.at[slot // 2], device_id=(sibling, tp), device_id_type=MESH,
        )

    def from_sibling(block):
        both = buf.at[0, pl.ds(0, 2 * S_DEV)]
        pltpu.make_async_remote_copy(
            src_ref=both, dst_ref=both, send_sem=sent.at[0], recv_sem=recv_sib.at[block],
            device_id=(sibling, tp), device_id_type=MESH,
        ).wait_recv()

    def to_right(kind, hops, p):
        return copy(kind, at(y_hi, -hops), p, right, tp)

    def to_left(kind, hops, p):
        return copy(kind, at(y_hi, hops), p, left, tp)

    def to_second(slot, p, steps):
        return copy(y_lo, slot, p, at(y_hi, steps), tp)

    def to_cross(slot, p):
        return copy(y_lo, slot, p, other_hi, pair)

    def to_pair(slot, p):
        return copy(kind_on, slot, p, ctx, pair)

    k_load = pltpu.make_async_copy(
        kv_ref.at[0, :, pl.ds(pl.multiple_of(x * HD, HD), HD)], part(0, ctx), load.at[3]
    )
    v_load = pltpu.make_async_copy(
        kv_ref.at[1, :, pl.ds(pl.multiple_of(x * HD, HD), HD)], own_v, load.at[0]
    )
    q_load = pltpu.make_async_copy(q_ref, q_rows, load.at[4])
    start_load = pltpu.make_async_copy(start_ref, starts, load.at[6])
    len_load = pltpu.make_async_copy(len_ref, lens, load.at[7])
    v_load.start()
    k_load.start()
    q_load.start()
    start_load.start()
    len_load.start()
    barrier = pltpu.get_barrier_semaphore()
    for to_ctx, to_tp in (
        (right, tp), (left, tp), (sibling, tp), (other_hi, pair), (ctx, pair),
        (ctx, x_right), (ctx, x_left), (ctx, x_far),
        (at(y_hi, 2), tp), (at(y_hi, -2), tp),
    ):
        pl.semaphore_signal(barrier, inc=1, device_id=(to_ctx, to_tp), device_id_type=MESH)
    for there, to_ctx in ((has_above, above), (has_below, below)):
        @pl.when(there)
        def _(to_ctx=to_ctx):
            pl.semaphore_signal(barrier, inc=1, device_id=(to_ctx, tp), device_id_type=MESH)

    v_load.wait()
    v_own = own_v[...].astype(jnp.float32)
    for half in range(2):
        turned = v_own[half * HD : (half + 1) * HD].T.astype(jnp.bfloat16)
        start = pl.multiple_of(ctx * S_DEV + half * HD, HD)
        buf[1, pl.ds(start, HD), :] = turned
    k_load.wait()
    pl.semaphore_wait(barrier, jnp.where(has_above & has_below, 12, 11))

    def start_near(kind):
        for p in range(2):
            to_right(kind, 0, p).start()
            to_left(kind, 0, 1 - p).start()

    @pl.when(y_hi == 0)
    def _():
        for p in range(2):
            to_second(ctx, p, 2).start()
            to_second(ctx, 1 - p, -2).start()
            to_cross(ctx, p).start()

    @pl.when(y_hi == 1)
    def _():
        start_near(0)

    for kind in range(2):
        to_sibling(kind, ctx).start()

    q_load.wait()
    for h in range(4):
        q_t[:, h * S_DEV : (h + 1) * S_DEV] = (
            q_rows[:, h * HD : (h + 1) * HD].astype(jnp.float32).T.astype(jnp.bfloat16)
        )

    @pl.when(y_hi == 0)
    def _():
        start_near(y_lo)

    @pl.when(y_hi == 1)
    def _():
        start_near(1)

    def low_ring(hops):
        def side(sign, p):
            slot = at(0, sign * hops)
            arrived(y_lo, slot, p)
            if hops == 2:
                copy(y_lo, slot, p, left if sign > 0 else right, tp).start()
                if (p == 0) == (sign < 0):
                    to_second(slot, p, -2 * sign).start()
            to_cross(slot, p).start()
            to_pair(slot, p).start()

        for p in range(2):
            side(-1, p)
            if hops < 4:
                side(1, 1 - p)
        for slot in low_slots(hops):
            to_sibling(y_lo, slot).start()

    def ring(hops):
        def side(kind, moving_right, p):
            arrived(kind, at(y_hi, -hops if moving_right else hops), p)
            last = 3 if (p == 0) == moving_right else 2
            if hops <= last:
                (to_right if moving_right else to_left)(kind, hops, p).start()

        kinds = range(2)
        if hops < 4:
            for kind in kinds:
                for k in range(2):
                    side(kind, True, k)
                    side(kind, False, 1 - k)
            for kind in kinds:
                to_sibling(kind, at(y_hi, -hops)).start()
                to_sibling(kind, at(y_hi, hops)).start()
        else:
            for kind in kinds:
                side(kind, True, 0)
                side(kind, False, 1)
                to_sibling(kind, at(y_hi, 4)).start()

    def low_slots(hops):
        if hops in (0, 4):
            return [at(0, hops)]
        return [at(0, -hops), at(0, hops)]

    def from_cross(hops):
        for p in (0, 1):
            for k, slot in enumerate(low_slots(hops)):
                q = p if k == 0 else 1 - p
                arrived(kind_on, slot, q)
                to_pair(slot, q).start()
        for slot in low_slots(hops):
            to_sibling(kind_on, slot).start()

    def from_pair(hops):
        for slot in low_slots(hops):
            arrived(kind_swap, slot, 0)
            arrived(kind_swap, slot, 1)
            to_sibling(kind_swap, slot).start()


    def slot_at(steps, same):
        return ((x + steps + 4) % 4) * 2 + (y_lo if same else 1 - y_lo)

    def quarter(slot, q):
        return att.at[slot, pl.ds(q * QUARTER, QUARTER)]

    def send(slot, q, to_tp):
        return pltpu.make_async_remote_copy(
            src_ref=quarter(slot, q), dst_ref=quarter(slot, q), send_sem=sent.at[0],
            recv_sem=x_recv.at[slot, q], device_id=(ctx, to_tp), device_id_type=MESH,
        )

    x_to_right = lambda slot, q: send(slot, q, x_right)
    x_to_left = lambda slot, q: send(slot, q, x_left)
    x_to_pair = lambda slot, q: send(slot, q, pair)

    def landed_at(slot, q):
        x_to_pair(slot, q).wait_recv()

    def edge_copy(k):
        to_ctx = above if k == 0 else below
        src = teacher_ref.at[pl.ds(TEACH - EDGE, EDGE)] if k == 0 else teacher_ref.at[pl.ds(0, EDGE)]
        dst = ext.at[pl.ds(0, EDGE)] if k == 0 else ext.at[pl.ds(EDGE + TEACH, EDGE)]
        return pltpu.make_async_remote_copy(
            src_ref=src, dst_ref=dst, send_sem=sent.at[0], recv_sem=edge_recv.at[k],
            device_id=(to_ctx, tp), device_id_type=MESH,
        )

    def grad_copy(k, half):
        part = pl.ds(half * (WIDTH // 2), WIDTH // 2)
        return pltpu.make_async_remote_copy(
            src_ref=edges.at[k, :, part], dst_ref=landed.at[k, :, part], send_sem=sent.at[0],
            recv_sem=edge_recv.at[2 + 2 * k + half], device_id=(above if k == 0 else below, tp),
            device_id_type=MESH,
        )

    def weight_load(slot):
        rows = pl.ds(pl.multiple_of(slot * DEPTH, DEPTH), DEPTH)
        return pltpu.make_async_copy(weight_ref.at[rows], weight.at[rows], load.at[5])

    student_load = pltpu.make_async_copy(student_ref, student, load.at[1])
    teacher_load = pltpu.make_async_copy(teacher_ref, ext.at[pl.ds(EDGE, TEACH)], load.at[2])
    def edge_and_loads():
        for k, there in ((0, has_above), (1, has_below)):
            @pl.when(there)
            def _(k=k):
                edge_copy(k).start()

        student_load.start()
        teacher_load.start()
        for slot in range(8):
            weight_load(slot).start()

    half_rows = 2 * S_DEV

    def score(block, c, masked=False):
        cols = slice(c * half_rows, (c + 1) * half_rows)
        keys = buf[0, pl.ds(pl.multiple_of(block * 2 * S_DEV, 2 * S_DEV), 2 * S_DEV), :]
        s = jnp.dot(keys, q_t[:, cols], preferred_element_type=jnp.float32)
        if masked:
            key_pos = lax.broadcasted_iota(jnp.int32, s.shape, 0)
            query_pos = lax.broadcasted_iota(jnp.int32, s.shape, 1) % S_DEV + core * S_DEV
            s = jnp.where(key_pos <= query_pos, s, LOW)
        scores[c] = s
        new_peak = jnp.max(s, axis=0, keepdims=True)
        if not masked:
            old = peak[:, cols]
            new_peak = jnp.maximum(old, new_peak)
            decay[:, cols] = jnp.exp2((old - new_peak) * EXP_SCALE)
        peak[:, cols] = new_peak

    def gather_values(block, c, first=False):
        cols = slice(c * half_rows, (c + 1) * half_rows)
        weights = jnp.exp2((scores[c] - peak[:, cols]) * EXP_SCALE)
        added = jnp.sum(weights, axis=0, keepdims=True)
        rounded = weights.astype(jnp.bfloat16)
        base = block * 2 * S_DEV
        product = None
        for k in range(2):
            parts = [
                buf[1, pl.ds(pl.multiple_of(base + k * S_DEV + g * HD, HD), HD), :]
                for g in range(2)
            ]
            values = jnp.concatenate(parts, axis=1)
            term = jnp.dot(
                values, rounded[k * S_DEV : (k + 1) * S_DEV], preferred_element_type=jnp.float32
            )
            product = term if product is None else product + term
        if first:
            total[:, cols] = added
            accum[:, cols] = product
        else:
            shrink = decay[:, cols]
            total[:, cols] = total[:, cols] * shrink + added
            accum[:, cols] = accum[:, cols] * shrink + product

    own_block = ctx // 2
    from_sibling(ctx // 2)
    score(own_block, 0, masked=True)
    score(own_block, 1, masked=True)
    gather_values(own_block, 0, first=True)
    total[:, half_rows:] = jnp.zeros((1, half_rows), jnp.float32)
    accum[:, half_rows:] = jnp.zeros((HD, half_rows), jnp.float32)
    decay[:, half_rows:] = jnp.ones((1, half_rows), jnp.float32)

    low_order = {2: (1, -1), 3: (1, 1), 4: (1, -2), 5: (1, 2), 7: (1, -3), 8: (1, 3), 9: (1, 4)}
    low_events = {
        1: [(low_ring, 2), (low_ring, 1), (low_ring, 3), (low_ring, 4)], 2: [(from_pair, 1)],
        4: [(from_pair, 2)], 7: [(from_pair, 3)], 8: [(from_pair, 4)],
    }
    high_order = {
        1: (1, -1), 2: (1, 1), 3: (2, 0), 4: (1, -2), 5: (1, 2), 6: (1, -3), 7: (1, 3), 8: (2, -1),
        9: (2, 1), 10: (2, -2), 11: (2, 2), 12: (1, 4), 13: (2, -3), 14: (2, 3), 15: (2, 4),
    }
    high_events = {
        1: [(ring, 1), (from_cross, 0)], 3: [(ring, 2), (from_pair, 0)],
        4: [(from_cross, 1), (from_cross, 2)], 6: [(ring, 3)], 7: [(from_cross, 3)],
        8: [(from_cross, 4), (from_pair, 1), (from_pair, 2)], 11: [(ring, 4)],
        12: [(from_pair, 3)], 13: [(from_pair, 4)],
    }

    def lookup(n, field):
        low = pick(n, [low_order.get(k, (0, 0))[field] for k in range(16)])
        high = pick(n, [high_order.get(k, (0, 0))[field] for k in range(16)])
        return jnp.where(y_hi == 0, low, high)

    def step(n, before):
        plane = lookup(n, 0)
        block_z = (z + lookup(n, 1) + N_Z) % N_Z
        for hi, events in ((0, low_events), (1, high_events)):
            @pl.when(y_hi == hi)
            def _(events=events):
                for k, todo in events.items():
                    @pl.when(n == k)
                    def _(todo=todo):
                        for action, hops in todo:
                            action(hops)

        @pl.when(n == 9)
        def _():
            edge_and_loads()

        block = jnp.where(plane == 2, block_z, y_hi * N_Z + block_z)
        here = plane > 0

        @pl.when(here)
        def _():
            from_sibling(block)

        def compute(prior):
            score(block, 0)
            gather_values(prior, 1)
            score(block, 1)
            gather_values(block, 0)
            return block

        return lax.cond(here & (block < own_block), compute, lambda prior: prior, before)

    last_block = lax.fori_loop(1, 16, step, own_block)
    def place_head(h):
        cols = slice(h * S_DEV, (h + 1) * S_DEV)
        att[tp, :, h * HD : (h + 1) * HD] = (accum[:, cols] / total[:, cols]).T.astype(jnp.bfloat16)

    place_head(0)
    place_head(1)
    gather_values(last_block, 1)
    place_head(2)
    place_head(3)


    for q in range(2):
        x_to_right(tp, q).start()
        x_to_left(tp, q).start()
        x_to_pair(tp, 2 + q).start()
    @pl.when(ctx == 0)
    def _():
        ext[:EDGE, :] = jnp.zeros((EDGE, WIDTH), jnp.bfloat16)
        landed[0] = jnp.zeros((HALO, WIDTH), jnp.float32)

    @pl.when(ctx == 31)
    def _():
        ext[EDGE + TEACH : WINDOW, :] = jnp.zeros((EDGE, WIDTH), jnp.bfloat16)
        landed[1] = jnp.zeros((HALO, WIDTH), jnp.float32)

    ext[WINDOW:, :] = jnp.zeros((ext.shape[0] - WINDOW, WIDTH), jnp.bfloat16)
    first = ctx * TEACH - EDGE
    start_load.wait()
    len_load.wait()
    start_row, len_row = starts[...], lens[...]
    row_pos = first + lax.broadcasted_iota(jnp.int32, (WINDOW, S_DEV), 0)
    inside = (row_pos >= start_row) & (row_pos < start_row + len_row)
    member_t[...] = jnp.where(inside, 1.0, 0.0).astype(jnp.bfloat16)
    for q in range(2):
        send(tp, q, x_far).start()
        x_to_pair(tp, q).start()
    wide_start = jnp.broadcast_to(start_row.astype(jnp.float32), (HD, S_DEV)).T[:, :1]
    wide_len = jnp.broadcast_to(len_row.astype(jnp.float32), (HD, S_DEV)).T
    counts[...] = 1.0 / wide_len
    col_pos = (first + lax.broadcasted_iota(jnp.int32, member.shape, 1)).astype(jnp.float32)
    inside = (col_pos >= wide_start) & (col_pos < wide_start + wide_len[:, :1])
    member[...] = jnp.where(inside, 1.0, 0.0).astype(jnp.bfloat16)
    student_load.wait()
    result[...] = student[...].astype(jnp.float32)

    def columns(j):
        return pl.ds(j * TILE, TILE)

    def multiply(slot):
        rows = pl.ds(pl.multiple_of(slot * DEPTH, DEPTH), DEPTH)

        result[...] += jnp.dot(att[slot], weight[rows, :], preferred_element_type=jnp.float32)

    prev, nxt = slot_at(-1, True), slot_at(1, True)
    far, far_other = slot_at(2, True), slot_at(2, False)
    prev_other, nxt_other = slot_at(-1, False), slot_at(1, False)

    for q in range(2):
        x_to_right(tp, 2 + q).start()
        x_to_left(tp, 2 + q).start()
    for q in (2, 3):
        landed_at(pair, q)
        x_to_right(pair, q).start()
        x_to_left(pair, q).start()
    pltpu.make_async_copy(weight_ref, weight, load.at[5]).wait()
    multiply(tp)
    for q in range(2):
        for slot in (prev, nxt):
            landed_at(slot, q)
            x_to_pair(slot, q).start()
    landed_at(prev, 2)
    x_to_right(prev, 2).start()
    landed_at(nxt, 3)
    x_to_left(nxt, 3).start()
    for q in range(2):
        landed_at(far, q)
        x_to_pair(far, q).start()
    teacher_load.wait()
    for k, there in ((0, has_below), (1, has_above)):
        @pl.when(there)
        def _(k=k):
            edge_copy(k).wait_recv()


    summed = jnp.dot(member[...], ext[...], preferred_element_type=jnp.float32)
    target[...] = summed * counts[:, :1]

    landed_at(pair, 0)
    landed_at(pair, 1)
    landed_at(prev_other, 2)
    x_to_right(prev_other, 2).start()
    landed_at(nxt_other, 3)
    x_to_left(nxt_other, 3).start()
    multiply(pair)
    landed_at(prev, 3)
    multiply(prev)
    landed_at(nxt, 2)
    multiply(nxt)
    for q in (2, 3):
        landed_at(far, q)
    multiply(far)
    for q in (3, 0, 1):
        landed_at(prev_other, q)
    multiply(prev_other)
    for q in (2, 0, 1):
        landed_at(nxt_other, q)
    multiply(nxt_other)
    for q in (2, 3, 0, 1):
        landed_at(far_other, q)
    last_rows = pl.ds(pl.multiple_of(far_other * DEPTH, DEPTH), DEPTH)

    for j in range(WIDTH // TILE):
        student32 = result[:, columns(j)] + jnp.dot(
            att[far_other], weight[last_rows, columns(j)], preferred_element_type=jnp.float32
        )
        student[:, columns(j)] = student32.astype(jnp.bfloat16)
        weighted = ((student32 - target[:, columns(j)]) * counts[:, :1]).astype(jnp.bfloat16)
        spread = jnp.dot(member_t[...], weighted, preferred_element_type=jnp.float32)
        edges[0, :, columns(j)] = spread[EDGE + TEACH : EDGE + TEACH + HALO]
        edges[1, :, columns(j)] = spread[EDGE - HALO : EDGE]
        result[:, columns(j)] = spread[EDGE : EDGE + S_DEV]
        target[: TEACH - S_DEV, columns(j)] = spread[EDGE + S_DEV : EDGE + TEACH]
        if j % 2 == 1:
            for k, there in ((0, has_above), (1, has_below)):
                @pl.when(there)
                def _(k=k, j=j):
                    grad_copy(k, j // 2).start()


    out_store = pltpu.make_async_copy(student, out_ref, load.at[0])
    out_store.start()
    ext[EDGE:S_DEV, :] = result[EDGE:, :].astype(jnp.bfloat16)
    rest = TEACH - S_DEV - EDGE
    ext[S_DEV : TEACH - EDGE, :] = target[:rest, :].astype(jnp.bfloat16)
    grad_stores = [
        pltpu.make_async_copy(ext.at[part], grad_ref.at[part], load.at[1 + k])
        for k, part in enumerate(
            (pl.ds(EDGE, TEACH - 2 * EDGE), pl.ds(0, EDGE), pl.ds(TEACH - EDGE, EDGE))
        )
    ]
    grad_stores[0].start()
    for k, there in ((0, has_below), (1, has_above)):
        @pl.when(there)
        def _(k=k):
            for half in range(2):
                grad_copy(k, half).wait_recv()

    low = result[:EDGE, :] + jnp.concatenate([landed[0], jnp.zeros_like(landed[0])], axis=0)
    ext[:EDGE, :] = low.astype(jnp.bfloat16)
    grad_stores[1].start()
    high = target[rest : rest + EDGE, :] + jnp.concatenate(
        [jnp.zeros_like(landed[1]), landed[1]], axis=0
    )
    ext[TEACH - EDGE : TEACH, :] = high.astype(jnp.bfloat16)
    grad_stores[2].start()

    out_store.wait()
    for store in grad_stores:
        store.wait()

    def all_sent(pieces):
        rows = weight.at[pl.ds(0, pieces * 16)]
        pltpu.make_async_remote_copy(
            src_ref=rows, dst_ref=rows, send_sem=sent.at[0], recv_sem=edge_recv.at[0],
            device_id=(sibling, tp), device_id_type=MESH,
        ).wait_send()

    for hi, pieces in ((0, 14 + 16 + 14 + 32 + 56), (1, 28 + 16 + 64 + 56)):
        inner = has_above & has_below

        @pl.when((y_hi == hi) & inner)
        def _(pieces=pieces):
            all_sent(pieces + 4)

        @pl.when((y_hi == hi) & ~inner)
        def _(pieces=pieces):
            all_sent(pieces + 2)


def place_kernel(rows_in, grad_in, out_ref, grad_ref, rows, grad, sems):
    pairs = []
    for source, middle, result in ((rows_in, rows, out_ref), (grad_in, grad, grad_ref)):
        for k in range(2):
            size = source.shape[0] // 2
            part = pl.ds(k * size, size)
            at = len(pairs)
            pairs.append((
                pltpu.make_async_copy(source.at[part], middle.at[part], sems.at[0, at]),
                pltpu.make_async_copy(middle.at[part], result.at[part], sems.at[1, at]),
            ))
    for fetch, _ in pairs:
        fetch.start()
    for fetch, store in pairs:
        fetch.wait()
        store.start()
    for _, store in pairs:
        store.wait()


def body(student_rows, queries, keys_values, out_weight, teacher_rows, span_start, span_len):
    anywhere = pl.BlockSpec(memory_space=pl.ANY)
    dma = pltpu.SemaphoreType.DMA
    bf16, f32 = jnp.bfloat16, jnp.float32
    wide = 4 * S_DEV
    results = (
        jax.ShapeDtypeStruct((S_DEV, WIDTH), bf16),
        jax.ShapeDtypeStruct((TEACH, WIDTH), bf16),
    )
    rows, grad = pl.pallas_call(
        layer_kernel,
        out_shape=results,
        in_specs=[anywhere] * 7,
        out_specs=(anywhere, anywhere),
        scratch_shapes=[
            pltpu.VMEM((2, 32 * S_DEV, HD), bf16),
            pltpu.VMEM((S_DEV, HD), bf16),
            pltpu.VMEM((S_DEV, DEPTH), bf16),
            pltpu.VMEM((HD, wide), bf16),
            pltpu.VMEM((2, 2 * S_DEV, wide // 2), f32),
            pltpu.VMEM((1, wide), f32),
            pltpu.VMEM((1, wide), f32),
            pltpu.VMEM((1, wide), f32),
            pltpu.VMEM((HD, wide), f32),
            pltpu.VMEM((8, S_DEV, DEPTH), bf16),
            pltpu.VMEM((8 * DEPTH, WIDTH), bf16),
            pltpu.VMEM((S_DEV, WIDTH), bf16),
            pltpu.VMEM((512, WIDTH), bf16),
            pltpu.VMEM((S_DEV, 512), bf16),
            pltpu.VMEM((WINDOW, S_DEV), bf16),
            pltpu.VMEM((S_DEV, WIDTH), f32),
            pltpu.VMEM((S_DEV, WIDTH), f32),
            pltpu.VMEM((S_DEV, HD), f32),
            pltpu.VMEM((2, HALO, WIDTH), f32),
            pltpu.VMEM((2, HALO, WIDTH), f32),
            pltpu.VMEM((1, S_DEV), jnp.int32),
            pltpu.VMEM((1, S_DEV), jnp.int32),
            dma((2, 32)), dma((16,)), dma((1,)), dma((8, 4)), dma((8,)), dma((6,)),
        ],
        compiler_params=pltpu.CompilerParams(
            collective_id=0, has_side_effects=True, vmem_limit_bytes=60 << 20
        ),
        name="layer",
    )(
        queries, keys_values, student_rows, out_weight, teacher_rows,
        span_start.reshape(1, S_DEV), span_len.reshape(1, S_DEV),
    )
    return pl.pallas_call(
        place_kernel,
        out_shape=results,
        in_specs=[anywhere] * 2,
        out_specs=(anywhere, anywhere),
        scratch_shapes=[
            pltpu.VMEM((S_DEV, WIDTH), bf16),
            pltpu.VMEM((TEACH, WIDTH), bf16),
            dma((2, 4)),
        ],
        compiler_params=pltpu.CompilerParams(vmem_limit_bytes=60 << 20),
        name="place",
    )(rows, grad)


def solution(mesh):
    return jax.shard_map(
        body,
        mesh=mesh,
        in_specs=(
            P("ctx", "tp"),
            P("ctx", "tp"),
            P(None, "ctx", None),
            P(None, "tp"),
            P("ctx", "tp"),
            P("ctx"),
            P("ctx"),
        ),
        out_specs=(P("ctx", "tp"), P("ctx", "tp")),
        check_vma=False,
    )
```
